32 devices in a mesh: ctx: 8 (over z, y), tp: 4 (over x, core).
Axes of the slice: x: 2, y: 2, z: 4, core: 2. Of those that a mesh axis runs over, the one named last changes fastest.
Arguments:
- query_one: bfloat16 [2048, 8192], P('ctx', 'tp'), may hold values from -6 to 6
- key_one: bfloat16 [2048, 8192], P('ctx', 'tp'), may hold values from -6 to 6
- value_one: bfloat16 [2048, 8192], P('ctx', 'tp'), may hold values from -6 to 6
- residual_in: bfloat16 [2048, 8192], P('ctx', 'tp'), may hold values from -50 to 50
- medium_taps: bfloat16 [128, 8192], P(None, 'tp'), may hold values from -0.5 to 0.5
- skip_one: float32 [8192], P('tp'), may hold values from -4 to 4
- norm_gain: float32 [8192], P('tp'), may hold values from 0.5 to 1.5
- query_two: bfloat16 [2048, 8192], P('ctx', 'tp'), may hold values from -6 to 6
- key_two: bfloat16 [2048, 8192], P('ctx', 'tp'), may hold values from -6 to 6
- residues: float32 [16, 8192], P(None, 'tp'), may hold values from -2 to 2
- decay_rates: float32 [16, 8192], P(None, 'tp'), may hold values from 0.00048828125 to 0.03
- skip_two: float32 [8192], P('tp'), may hold values from -4 to 4
Outputs:
- residual_out: bfloat16 [2048, 8192], P('ctx', 'tp')
- long_output: bfloat16 [2048, 8192], P('ctx', 'tp')
The draws below stay inside these ranges and needn't reach their ends.
All inputs are finite; a program needn't handle non-finite values.
Results may differ from the reference program's by a relative error of at most 0.013.
Values may be sent and summed in bfloat16 or wider, within the bound.
A program may use at most 128 MiB of HBM per device.

```python
import math
import jax
import jax.numpy as jnp
from jax import lax

D = 8192
TAPS = 128
MODES = 16
TOKENS = 2048


def draw_residual_in(key, part):
    key_rows, key_cols, key_base = jax.random.split(key, 3)
    row_scale = jnp.exp(jax.random.uniform(key_rows, (TOKENS, 1), jnp.float32, math.log(0.3), math.log(3.0)))
    column_ramp = 0.5 * jnp.exp(math.log(3.0) * jnp.arange(D).astype(jnp.float32) / (D - 1))
    column_rough = jnp.exp(jax.random.uniform(key_cols, (D,), jnp.float32, -0.6, 0.6))
    base_values = jax.random.normal(key_base, (TOKENS, D), jnp.float32)
    base_values = jnp.clip(base_values, -6.0, 6.0)
    return jnp.clip(base_values * row_scale * column_ramp * column_rough, -50.0, 50.0).astype(jnp.bfloat16)


def steps_of(own_key, extent, pieces, smallest, largest):
    level = 1.0
    for position, parts in pieces:
        heights = jax.random.uniform(jax.random.fold_in(jax.random.fold_in(own_key, 6), position), (parts,), jnp.float32, smallest / len(pieces), largest / len(pieces))
        level = level * jnp.repeat(jnp.exp(heights), extent[position] // parts).reshape((-1,) + (1,) * (len(extent) - 1 - position))
    return level


def noise(stream_key, extent, spread, limit, cuts=(), held_as=jnp.bfloat16):
    values = jax.random.normal(stream_key, extent, jnp.float32) * spread
    if len(cuts) > 0:
        values = steps_of(stream_key, extent, cuts, -0.22, 0.18) * values
    return jnp.clip(values, min=-limit, max=limit).astype(held_as)


def setup_inputs(seed: int = 0) -> dict:
    seeds = jax.random.split(jax.random.key(seed), 13)
    query_one = noise(seeds[0], (TOKENS, D), 1.0, 6.0, ((0, 8), (1, 4)))
    key_one = noise(seeds[1], (TOKENS, D), 1.0, 6.0, ((0, 8), (1, 4)))
    value_one = noise(seeds[2], (TOKENS, D), 1.0, 6.0, ((0, 8), (1, 4)))
    residual_in = draw_residual_in(jax.random.fold_in(seeds[12], 71), 0)
    medium_taps = noise(seeds[4], (TAPS, D), TAPS ** -0.5, 0.5, ((1, 4),))
    skip_one = noise(seeds[5], (D,), 1.0, 4.0, ((0, 4),), jnp.float32)
    norm_gain = jnp.clip(1.0 + 0.1 * jax.random.normal(seeds[6], (D,), jnp.float32), 0.5, 1.5)
    query_two = noise(seeds[7], (TOKENS, D), 1.0, 6.0, ((0, 8), (1, 4)))
    key_two = noise(seeds[8], (TOKENS, D), 1.0, 6.0, ((0, 8), (1, 4)))
    residues = noise(seeds[9], (MODES, D), 0.35, 2.0, ((1, 4),), jnp.float32)
    decay_rates = jnp.clip(jnp.exp(math.log(0.03) - 4.118061 * jax.random.uniform(seeds[10], (MODES, D), jnp.float32) ** steps_of(seeds[10], (MODES, D), ((1, 4),), -0.2, 0.2)), 0.00048828125, 0.03)
    skip_two = noise(seeds[11], (D,), 1.0, 4.0, ((0, 4),), jnp.float32)
    return dict(query_one=query_one, key_one=key_one, value_one=value_one, residual_in=residual_in, medium_taps=medium_taps, skip_one=skip_one, norm_gain=norm_gain, query_two=query_two, key_two=key_two, residues=residues, decay_rates=decay_rates, skip_two=skip_two)


def modal_taps(local_residues, local_rates, offsets):
    running = jnp.zeros((offsets.shape[0], local_residues.shape[1]), jnp.float32)
    for mode_index in range(local_residues.shape[0]):
        running = running + local_residues[mode_index] * jnp.sqrt(local_rates[mode_index]) * jnp.exp(-local_rates[mode_index] * offsets[:, None])
    return running

def reference(query_one, key_one, value_one, residual_in, medium_taps, skip_one, norm_gain, query_two, key_two, residues, decay_rates, skip_two):
    product_one = (key_one.astype(jnp.float32) * value_one.astype(jnp.float32)).astype(jnp.bfloat16)
    padded = jnp.concatenate([jnp.zeros((TAPS - 1, D), jnp.bfloat16), product_one], axis=0)

    def add_tap(tap_index, running):
        shifted = lax.dynamic_slice_in_dim(padded, (TAPS - 1 - tap_index).astype(jnp.int32), TOKENS, 0)
        return running + medium_taps[tap_index].astype(jnp.float32) * shifted.astype(jnp.float32)
    filtered = lax.fori_loop(0, TAPS, add_tap, jnp.zeros((TOKENS, D), jnp.float32))
    residual_out = (residual_in.astype(jnp.float32) + query_one.astype(jnp.float32) * (filtered + skip_one * product_one.astype(jnp.float32))).astype(jnp.bfloat16)
    widened = residual_out.astype(jnp.float32)
    mean_sq = lax.optimization_barrier(jnp.mean(widened * widened, axis=1, keepdims=True))
    value_two = (key_two.astype(jnp.float32) * widened * lax.rsqrt(mean_sq + 1e-05) * norm_gain).astype(jnp.bfloat16).astype(jnp.float32)

    def convolve_block(block_index):
        start_col = (block_index * 256).astype(jnp.int32)
        signal = lax.dynamic_slice_in_dim(value_two, start_col, 256, 1)
        local_residues = lax.dynamic_slice_in_dim(residues, start_col, 256, 1)
        local_rates = lax.dynamic_slice_in_dim(decay_rates, start_col, 256, 1)
        offsets = jnp.arange(TOKENS).astype(jnp.float32)
        taps_long = modal_taps(local_residues, local_rates, offsets)
        product_spectrum = jnp.fft.rfft(signal, n=2 * TOKENS, axis=0) * jnp.fft.rfft(taps_long, n=2 * TOKENS, axis=0)
        return jnp.fft.irfft(product_spectrum, n=2 * TOKENS, axis=0)[:TOKENS]
    blocks = lax.map(convolve_block, jnp.arange(D // 256, dtype=jnp.int32))
    mixed_two = jnp.transpose(blocks, (1, 0, 2)).reshape(TOKENS, D)
    long_output = (query_two.astype(jnp.float32) * (mixed_two + skip_two * value_two)).astype(jnp.bfloat16)
    return (residual_out, long_output)
```

```python
import functools

import jax
import jax.numpy as jnp
import ml_dtypes
import numpy as np
from jax import lax
from jax.experimental import pallas as pl
from jax.experimental.pallas import tpu as pltpu
from jax.sharding import PartitionSpec as P

F32 = jnp.float32
BF16 = jnp.bfloat16
MESH = pl.DeviceIdType.MESH
LANES = 128
CHUNK = 512


def half_bin_tables(period, rows_in, out_from, out_to):
    bins = np.arange(period // 2)[:, None] + 0.5
    angle = 2.0 * np.pi / period * bins * np.arange(period)[None, :]
    forward = np.concatenate([np.cos(angle), -np.sin(angle)], axis=0)[:, :rows_in]
    inverse = np.concatenate([np.cos(angle), -np.sin(angle)], axis=0).T[out_from:out_to] * (2.0 / period)
    return [x.astype(ml_dtypes.bfloat16).astype(np.float32) for x in (forward, inverse)]


def dot(left, right):
    return jnp.dot(left, right, preferred_element_type=F32)


def complex_product(x, h):
    half = x.shape[0] // 2
    xr, xi, hr, hi = x[:half], x[half:], h[:half], h[half:]
    return jnp.concatenate([xr * hr - xi * hi, xr * hi + xi * hr], axis=0).astype(BF16)


def kernel(
    n, tp_n,
    q1_h, k1_h, v1_h, res_h, taps_h, skip1, gain, q2_h, k2_h, residues, rates, skip2,
    fm_h, gm_h, fl_h, gl_h,
    rout_h, lout_h,
    q1, k1, v1, res, taps, q2, k2, fm32, gm32, fl32, gl32, fm, gm, fl, gl,
    buf, spec_m, spec_l, hbuf, rout, v2, loc, obuf,
    sq_acc, sq_send, sq_recv, scale, state, carry, st_send, st_recv,
    in_sem, out_sem, halo_send, halo_recv, sq_ssem, sq_rsem, st_ssem, st_rsem,
):
    T, C = q1.shape
    K = taps.shape[0]
    M = residues.shape[0]
    groups = C // LANES
    chunks = C // CHUNK
    steps = (n - 1).bit_length()
    d = lax.axis_index("ctx")
    t = lax.axis_index("tp")

    def lane(g):
        return pl.ds(pl.multiple_of(g * LANES, LANES), LANES)

    def cols(j):
        return pl.ds(pl.multiple_of(j * CHUNK, CHUNK), CHUNK)

    pairs = [
        (k1_h, k1), (v1_h, v1), (fm_h, fm32), (taps_h, taps), (gm_h, gm32), (q1_h, q1), (res_h, res),
        (fl_h, fl32), (k2_h, k2), (gl_h, gl32), (q2_h, q2),
    ]
    loads = [pltpu.make_async_copy(a, b, in_sem.at[i]) for i, (a, b) in enumerate(pairs)]
    for load in loads:
        load.start()

    barrier = pltpu.get_barrier_semaphore()
    shifts = [1 << i for i in range(steps)]
    for s in shifts:
        @pl.when(d + s < n)
        def _(s=s):
            pl.semaphore_signal(barrier, inc=1, device_id=(d + s, t), device_id_type=MESH)

        @pl.when(d >= s)
        def _(s=s):
            pl.semaphore_signal(barrier, inc=1, device_id=(d - s, t), device_id_type=MESH)
    for o in range(1, tp_n):
        pl.semaphore_signal(barrier, inc=1, device_id=(d, lax.rem(t + o, tp_n)), device_id_type=MESH)
    peers = tp_n - 1
    for s in shifts:
        peers = peers + (d + s < n).astype(jnp.int32) + (d >= s).astype(jnp.int32)
    pl.semaphore_wait(barrier, peers)

    def halo(j):
        c = pl.ds(j * CHUNK, CHUNK)
        return pltpu.make_async_remote_copy(
            src_ref=buf.at[pl.ds(T, K), c], dst_ref=buf.at[pl.ds(0, K), c],
            send_sem=halo_send.at[j], recv_sem=halo_recv.at[j],
            device_id=(lax.rem(d + 1, n), t), device_id_type=MESH)

    def product(row, j):
        c = pl.ds(j * CHUNK, CHUNK)
        r = pl.ds(row, K)
        buf[pl.ds(K + row, K), c] = (k1[r, c].astype(F32) * v1[r, c].astype(F32)).astype(BF16)

    loads[0].wait()
    loads[1].wait()
    for j in range(chunks):
        product(T - K, j)

        @pl.when(d + 1 < n)
        def _(j=j):
            halo(j).start()
    for j in range(chunks):
        product(0, j)

    @pl.when(d == 0)
    def _():
        buf[pl.ds(0, K), :] = jnp.zeros((K, C), BF16)

    for i in range(2, 7):
        loads[i].wait()
    fm[...] = fm32[...].astype(BF16)
    gm[...] = gm32[...].astype(BF16)

    def medium(row, j):
        c = cols(j)
        r = pl.ds(row, K)
        x = dot(fm[...], buf[pl.ds(row, 2 * K), c])
        filtered = dot(gm[...], complex_product(x, spec_m[:, c]))
        mixed = filtered + skip1[:, c] * buf[pl.ds(K + row, K), c].astype(F32)
        out = (res[r, c].astype(F32) + q1[r, c].astype(F32) * mixed).astype(BF16)
        rout[r, c] = out
        wide = out.astype(F32)
        square = wide * wide
        total = sq_acc[...]
        for i in range(CHUNK // LANES):
            total = total + square[:, i * LANES:(i + 1) * LANES]
        sq_acc[...] = total

    def send_squares(half):
        summed = jnp.sum(sq_acc[...], axis=1, keepdims=True)
        sq_send[half] = jnp.broadcast_to(summed, (K, LANES)).T[:8]
        for o in range(1, tp_n):
            squares(half, o).start()

    def squares(half, o):
        return pltpu.make_async_remote_copy(
            src_ref=sq_send.at[half], dst_ref=sq_recv.at[half, o - 1],
            send_sem=sq_ssem.at[half, o - 1], recv_sem=sq_rsem.at[half, o - 1],
            device_id=(d, lax.rem(t + o, tp_n)), device_id_type=MESH)

    def take_squares(half):
        total = sq_send[half]
        for o in range(1, tp_n):
            squares(half, o).wait()
            total = total + sq_recv[half, o - 1]
        root = lax.rsqrt(total * (1.0 / (C * tp_n)) + 1e-05)
        scale[...] = jnp.concatenate([root] * (K // 8), axis=0).T

    def mode_rows(g, offset, sign):
        sub = lax.broadcasted_iota(jnp.int32, (8, LANES), 0).astype(F32) * sign + offset
        eight, first = [], []
        for m in range(M):
            rate = jnp.broadcast_to(rates[pl.ds(m, 1), lane(g)], (8, LANES))
            eight.append(jnp.exp(rate * -8.0))
            first.append(jnp.exp(-rate * sub))
        return eight, first

    def weight(g, m):
        rate = rates[pl.ds(m, 1), lane(g)]
        return residues[pl.ds(m, 1), lane(g)] * jnp.sqrt(rate)

    def tree_sum(terms):
        while len(terms) > 1:
            terms = [a + b for a, b in zip(terms[::2], terms[1::2])] + terms[len(terms) // 2 * 2:]
        return terms[0]

    def next_rows(terms, eight):
        top = tree_sum(terms)
        terms = [p * a for p, a in zip(terms, eight)]
        bottom = tree_sum(terms)
        return jnp.concatenate([top, bottom], axis=0), [p * a for p, a in zip(terms, eight)]

    def normed(half, g, _):
        c = lane(g)
        eight, first = mode_rows(g, 7.0, -1.0)
        held = [jnp.zeros((8, LANES), F32)] * M
        for i in range(K // 16):
            r = pl.ds(half * K + i * 16, 16)
            value = (k2[r, c].astype(F32) * rout[r, c].astype(F32) * scale[pl.ds(i * 16, 16), :] * gain[:, c]).astype(BF16)
            v2[r, c] = value
            wide = value.astype(F32)
            held = [h * a + wide[:8] for h, a in zip(held, eight)]
            held = [h * a + wide[8:] for h, a in zip(held, eight)]
        for m in range(M):
            part = jnp.sum(held[m] * first[m], axis=0, keepdims=True)
            row = pl.ds(m, 1)
            if half == 0:
                state[row, c] = state[row, c] + jnp.exp(rates[row, c] * -float(K)) * part
            else:
                state[row, c] = part
        return 0

    def medium_spectrum(j, _):
        c = cols(j)
        spec_m[:, c] = dot(fm[:, :K], taps[:, c])
        medium(K, j)
        return 0

    sq_acc[...] = jnp.zeros_like(sq_acc)
    lax.fori_loop(0, chunks, medium_spectrum, 0)
    send_squares(1)

    def long_taps(g, _):
        eight, first = mode_rows(g, 0.0, 1.0)
        terms = [first[m] * weight(g, m) for m in range(M)]
        for i in range(T // 16):
            rows, terms = next_rows(terms, eight)
            hbuf[pl.ds(i * 16, 16), lane(g)] = rows.astype(BF16)
        return 0

    lax.fori_loop(0, groups, long_taps, 0)
    loads[7].wait()
    fl[...] = fl32[...].astype(BF16)

    def long_spectrum(j, _):
        spec_l[:, cols(j)] = dot(fl[...], hbuf[:, cols(j)])
        return 0

    lax.fori_loop(0, chunks, long_spectrum, 0)
    loads[8].wait()
    take_squares(1)
    lax.fori_loop(0, groups, functools.partial(normed, 1), 0)

    sq_acc[...] = jnp.zeros_like(sq_acc)
    for j in range(chunks):
        @pl.when(d >= 1)
        def _(j=j):
            halo(j).wait_recv()
        medium(0, j)
    send_squares(0)
    rout_copy = pltpu.make_async_copy(rout, rout_h, out_sem.at[chunks])
    rout_copy.start()
    take_squares(0)
    lax.fori_loop(0, groups, functools.partial(normed, 0), 0)
    loads[9].wait()
    gl[...] = gl32[...].astype(BF16)
    loads[10].wait()

    def hop(i):
        return pltpu.make_async_remote_copy(
            src_ref=st_send.at[i], dst_ref=st_recv.at[i],
            send_sem=st_ssem.at[i], recv_sem=st_rsem.at[i],
            device_id=(lax.rem(d + shifts[i], n), t), device_id_type=MESH)

    def inside(j, _):
        c = cols(j)
        y = complex_product(dot(fl[...], v2[:, c]), spec_l[:, c])
        loc[:, c] = dot(gl[...], y) + skip2[:, c] * v2[:, c].astype(F32)
        return 0

    carry[...] = jnp.zeros_like(carry)
    done = 0
    for i, s in enumerate(shifts):
        st_send[i] = state[...].astype(BF16)

        @pl.when(d + s < n)
        def _(i=i):
            hop(i).start()
        upto = chunks * (i + 1) // steps
        lax.fori_loop(done, upto, inside, 0)
        done = upto

        @pl.when(d >= s)
        def _(i=i, s=s):
            hop(i).wait_recv()
            arrived = st_recv[i].astype(F32)
            rate = rates[...]
            carry[...] += jnp.exp(rate * -float(T * (s - 1))) * arrived
            state[...] += jnp.exp(rate * -float(T * s)) * arrived

    def finish(g, _):
        c = lane(g)
        eight, first = mode_rows(g, 1.0, 1.0)
        terms = [first[m] * (weight(g, m) * carry[pl.ds(m, 1), c]) for m in range(M)]
        for i in range(T // 16):
            r = pl.ds(i * 16, 16)
            rows, terms = next_rows(terms, eight)
            obuf[r, c] = (q2[r, c].astype(F32) * (loc[r, c] + rows)).astype(BF16)
        return 0

    out_copies = []
    per = groups // chunks
    for j in range(chunks):
        lax.fori_loop(j * per, (j + 1) * per, finish, 0)
        c = pl.ds(j * CHUNK, CHUNK)
        copy = pltpu.make_async_copy(obuf.at[:, c], lout_h.at[:, c], out_sem.at[j])
        copy.start()
        out_copies.append(copy)

    for j in range(chunks):
        @pl.when(d + 1 < n)
        def _(j=j):
            halo(j).wait_send()
    for i, s in enumerate(shifts):
        @pl.when(d + s < n)
        def _(i=i):
            hop(i).wait_send()
    rout_copy.wait()
    for copy in out_copies:
        copy.wait()


def on_device(n, tp_n, q1, k1, v1, res, taps, skip1, gain, q2, k2, residues, rates, skip2):
    T, C = q1.shape
    K = taps.shape[0]
    M = residues.shape[0]
    assert T == 2 * K and C % CHUNK == 0
    chunks = C // CHUNK
    steps = (n - 1).bit_length()
    fm, gm = half_bin_tables(2 * K, 2 * K, K, 2 * K)
    fl, gl = half_bin_tables(2 * T, T, 0, T)
    hbm = pl.BlockSpec(memory_space=pl.ANY)
    vmem = pl.BlockSpec(memory_space=pltpu.VMEM)
    wide = pltpu.VMEM((T, C), BF16)
    return pl.pallas_call(
        functools.partial(kernel, n, tp_n),
        out_shape=[jax.ShapeDtypeStruct((T, C), BF16)] * 2,
        in_specs=[hbm] * 5 + [vmem] * 2 + [hbm] * 2 + [vmem] * 3 + [hbm] * 4,
        out_specs=[hbm] * 2,
        scratch_shapes=[
            wide, wide, wide, wide, pltpu.VMEM((K, C), BF16), wide, wide,
            pltpu.VMEM(fm.shape, F32), pltpu.VMEM(gm.shape, F32),
            pltpu.VMEM(fl.shape, F32), pltpu.VMEM(gl.shape, F32),
            pltpu.VMEM(fm.shape, BF16), pltpu.VMEM(gm.shape, BF16),
            pltpu.VMEM(fl.shape, BF16), pltpu.VMEM(gl.shape, BF16),
            pltpu.VMEM((T + K, C), BF16),
            pltpu.VMEM((2 * K, C), F32),
            pltpu.VMEM((2 * T, C), F32),
            wide, wide, wide,
            pltpu.VMEM((T, C), F32),
            wide,
            pltpu.VMEM((K, LANES), F32),
            pltpu.VMEM((2, 8, K), F32),
            pltpu.VMEM((2, tp_n - 1, 8, K), F32),
            pltpu.VMEM((K, LANES), F32),
            pltpu.VMEM((M, C), F32),
            pltpu.VMEM((M, C), F32),
            pltpu.VMEM((steps, M, C), BF16),
            pltpu.VMEM((steps, M, C), BF16),
            pltpu.SemaphoreType.DMA((11,)),
            pltpu.SemaphoreType.DMA((chunks + 1,)),
            pltpu.SemaphoreType.DMA((chunks,)),
            pltpu.SemaphoreType.DMA((chunks,)),
            pltpu.SemaphoreType.DMA((2, tp_n - 1)),
            pltpu.SemaphoreType.DMA((2, tp_n - 1)),
            pltpu.SemaphoreType.DMA((steps,)),
            pltpu.SemaphoreType.DMA((steps,)),
        ],
        compiler_params=pltpu.CompilerParams(
            collective_id=0, has_side_effects=True, vmem_limit_bytes=56 * 2**20),
        cost_estimate=pl.CostEstimate(
            flops=2 * 620000 * C, bytes_accessed=10 * T * C * 2, transcendentals=M * C * 16),
    )(q1, k1, v1, res, taps, skip1.reshape(1, C), gain.reshape(1, C), q2, k2, residues, rates,
      skip2.reshape(1, C), jnp.asarray(fm), jnp.asarray(gm), jnp.asarray(fl), jnp.asarray(gl))


def solution(mesh):
    rows = P("ctx", "tp")
    in_specs = (
        rows, rows, rows, rows, P(None, "tp"), P("tp"), P("tp"), rows, rows,
        P(None, "tp"), P(None, "tp"), P("tp"),
    )
    return jax.shard_map(
        functools.partial(on_device, mesh.shape["ctx"], mesh.shape["tp"]),
        mesh=mesh, in_specs=in_specs, out_specs=(rows, rows), check_vma=False)
```

```python
import functools

import jax
import jax.numpy as jnp
import ml_dtypes
import numpy as np
from jax import lax
from jax.experimental import pallas as pl
from jax.experimental.pallas import tpu as pltpu
from jax.sharding import PartitionSpec as P

F32 = jnp.float32
BF16 = jnp.bfloat16
MESH = pl.DeviceIdType.MESH
LANES = 128
CHUNK = 512


def half_bin_tables(period, rows_in, out_from, out_to):
    bins = np.arange(period // 2)[:, None] + 0.5
    angle = 2.0 * np.pi / period * bins * np.arange(period)[None, :]
    forward = np.concatenate([np.cos(angle), -np.sin(angle)], axis=0)[:, :rows_in]
    inverse = np.concatenate([np.cos(angle), -np.sin(angle)], axis=0).T[out_from:out_to] * (2.0 / period)
    return [x.astype(ml_dtypes.bfloat16).astype(np.float32) for x in (forward, inverse)]


def dot(left, right):
    return jnp.dot(left, right, preferred_element_type=F32)


def complex_product(x, h):
    half = x.shape[0] // 2
    xr, xi, hr, hi = x[:half], x[half:], h[:half], h[half:]
    return jnp.concatenate([xr * hr - xi * hi, xr * hi + xi * hr], axis=0).astype(BF16)


def kernel(
    n, tp_n,
    q1_h, k1_h, v1_h, res_h, taps_h, skip1, gain, q2_h, k2_h, residues, rates, skip2,
    fm_h, gm_h, fl_h, gl_h,
    rout_h, lout_h,
    q1, k1, v1, res, taps, q2, k2, fm32, gm32, fl32, gl32, fm, gm, fl, gl,
    buf, spec_m, spec_l, hbuf, rout, v2, loc, obuf,
    sq_acc, sq_send, sq_recv, scale, eight_t, weight_t, up_t, down_t, low, state, carry, st_send, st_recv,
    in_sem, out_sem, halo_send, halo_recv, sq_ssem, sq_rsem, st_ssem, st_rsem,
):
    T, C = q1.shape
    K = taps.shape[0]
    M = residues.shape[0]
    groups = C // LANES
    chunks = C // CHUNK
    steps = (n - 1).bit_length()
    d = lax.axis_index("ctx")
    t = lax.axis_index("tp")

    def lane(g):
        return pl.ds(pl.multiple_of(g * LANES, LANES), LANES)

    def cols(j):
        return pl.ds(pl.multiple_of(j * CHUNK, CHUNK), CHUNK)

    pairs = [
        (k1_h, k1), (v1_h, v1), (fm_h, fm32), (taps_h, taps), (gm_h, gm32), (q1_h, q1), (res_h, res),
        (fl_h, fl32), (k2_h, k2), (gl_h, gl32), (q2_h, q2),
    ]
    loads = [pltpu.make_async_copy(a, b, in_sem.at[i]) for i, (a, b) in enumerate(pairs)]
    for load in loads:
        load.start()

    barrier = pltpu.get_barrier_semaphore()
    shifts = [1 << i for i in range(steps)]
    for s in shifts:
        @pl.when(d + s < n)
        def _(s=s):
            pl.semaphore_signal(barrier, inc=1, device_id=(d + s, t), device_id_type=MESH)

        @pl.when(d >= s)
        def _(s=s):
            pl.semaphore_signal(barrier, inc=1, device_id=(d - s, t), device_id_type=MESH)
    for o in range(1, tp_n):
        pl.semaphore_signal(barrier, inc=1, device_id=(d, lax.rem(t + o, tp_n)), device_id_type=MESH)
    def halo(j):
        c = pl.ds(j * CHUNK, CHUNK)
        return pltpu.make_async_remote_copy(
            src_ref=buf.at[pl.ds(T, K), c], dst_ref=buf.at[pl.ds(0, K), c],
            send_sem=halo_send.at[j], recv_sem=halo_recv.at[j],
            device_id=(lax.rem(d + 1, n), t), device_id_type=MESH)

    def product(row, j):
        c = pl.ds(j * CHUNK, CHUNK)
        r = pl.ds(row, K)
        buf[pl.ds(K + row, K), c] = (k1[r, c].astype(F32) * v1[r, c].astype(F32)).astype(BF16)

    loads[0].wait()
    loads[1].wait()
    for j in range(chunks):
        product(T - K, j)
    peers = tp_n - 1
    for s in shifts:
        peers = peers + (d + s < n).astype(jnp.int32) + (d >= s).astype(jnp.int32)
    pl.semaphore_wait(barrier, peers)
    for j in range(chunks):
        @pl.when(d + 1 < n)
        def _(j=j):
            halo(j).start()
    for j in range(chunks):
        product(0, j)

    @pl.when(d == 0)
    def _():
        buf[pl.ds(0, K), :] = jnp.zeros((K, C), BF16)

    for i in range(2, 7):
        loads[i].wait()
    fm[...] = fm32[...].astype(BF16)
    gm[...] = gm32[...].astype(BF16)

    def medium(row, j):
        c = cols(j)
        r = pl.ds(row, K)
        x = dot(fm[...], buf[pl.ds(row, 2 * K), c])
        filtered = dot(gm[...], complex_product(x, spec_m[:, c]))
        mixed = filtered + skip1[:, c] * buf[pl.ds(K + row, K), c].astype(F32)
        out = (res[r, c].astype(F32) + q1[r, c].astype(F32) * mixed).astype(BF16)
        rout[r, c] = out
        wide = out.astype(F32)
        square = wide * wide
        total = sq_acc[...]
        for i in range(CHUNK // LANES):
            total = total + square[:, i * LANES:(i + 1) * LANES]
        sq_acc[...] = total

    def send_squares(half):
        summed = jnp.sum(sq_acc[...], axis=1, keepdims=True)
        sq_send[half] = jnp.broadcast_to(summed, (K, LANES)).T[:8]
        for o in range(1, tp_n):
            squares(half, o).start()

    def squares(half, o):
        return pltpu.make_async_remote_copy(
            src_ref=sq_send.at[half], dst_ref=sq_recv.at[half, o - 1],
            send_sem=sq_ssem.at[half, o - 1], recv_sem=sq_rsem.at[half, o - 1],
            device_id=(d, lax.rem(t + o, tp_n)), device_id_type=MESH)

    def take_squares(half):
        total = sq_send[half]
        for o in range(1, tp_n):
            squares(half, o).wait()
            total = total + sq_recv[half, o - 1]
        root = lax.rsqrt(total * (1.0 / (C * tp_n)) + 1e-05)
        scale[...] = jnp.concatenate([root] * (K // 8), axis=0).T

    def mode_tables(g, _):
        c = lane(g)
        sub = lax.broadcasted_iota(jnp.int32, (8, LANES), 0).astype(F32)
        rate = rates[:, c]
        eight_t[:, c] = jnp.exp(rate * -8.0)
        weight_t[:, c] = residues[:, c] * jnp.sqrt(rate)
        for m in range(M):
            row = jnp.broadcast_to(rates[pl.ds(m, 1), c], (8, LANES))
            up_t[pl.ds(8 * m, 8), c] = jnp.exp(-row * sub)
            down_t[pl.ds(8 * m, 8), c] = jnp.exp(-row * (7.0 - sub))
        return 0

    def eights(c):
        return [jnp.broadcast_to(eight_t[pl.ds(m, 1), c], (8, LANES)) for m in range(M)]

    def first_rows(factor, c):
        return [up_t[pl.ds(8 * m, 8), c] * factor[pl.ds(m, 1), c] for m in range(M)]

    def tree_sum(terms):
        while len(terms) > 1:
            terms = [a + b for a, b in zip(terms[::2], terms[1::2])] + terms[len(terms) // 2 * 2:]
        return terms[0]

    def next_rows(terms, eight):
        top = tree_sum(terms)
        terms = [p * a for p, a in zip(terms, eight)]
        bottom = tree_sum(terms)
        return jnp.concatenate([top, bottom], axis=0), [p * a for p, a in zip(terms, eight)]

    def normed(half, g, _):
        c = lane(g)
        eight = eights(c)
        held = [jnp.zeros((8, LANES), F32)] * M
        for i in range(K // 16):
            r = pl.ds(half * K + i * 16, 16)
            value = (k2[r, c].astype(F32) * rout[r, c].astype(F32) * scale[pl.ds(i * 16, 16), :] * gain[:, c]).astype(BF16)
            v2[r, c] = value
            wide = value.astype(F32)
            held = [h * a + wide[:8] for h, a in zip(held, eight)]
            held = [h * a + wide[8:] for h, a in zip(held, eight)]
        into = low if half == 0 else state
        for m in range(M):
            into[pl.ds(m, 1), c] = jnp.sum(held[m] * down_t[pl.ds(8 * m, 8), c], axis=0, keepdims=True)
        return 0

    def medium_spectrum(j, _):
        c = cols(j)
        spec_m[:, c] = dot(fm[:, :K], taps[:, c])
        medium(K, j)
        return 0

    sq_acc[...] = jnp.zeros_like(sq_acc)
    lax.fori_loop(0, chunks, medium_spectrum, 0)
    send_squares(1)

    def long_taps(g, _):
        c = lane(g)
        eight = eights(c)
        terms = first_rows(weight_t, c)
        for i in range(T // 16):
            rows, terms = next_rows(terms, eight)
            hbuf[pl.ds(i * 16, 16), c] = rows.astype(BF16)
        return 0

    lax.fori_loop(0, groups, mode_tables, 0)
    lax.fori_loop(0, groups, long_taps, 0)
    loads[7].wait()
    fl[...] = fl32[...].astype(BF16)

    def long_spectrum(j, _):
        spec_l[:, cols(j)] = dot(fl[...], hbuf[:, cols(j)])
        return 0

    lax.fori_loop(0, chunks, long_spectrum, 0)
    loads[8].wait()
    take_squares(1)
    lax.fori_loop(0, groups, functools.partial(normed, 1), 0)

    sq_acc[...] = jnp.zeros_like(sq_acc)
    for j in range(chunks):
        @pl.when(d >= 1)
        def _(j=j):
            halo(j).wait_recv()
        medium(0, j)
    send_squares(0)
    rout_copy = pltpu.make_async_copy(rout, rout_h, out_sem.at[chunks])
    rout_copy.start()
    take_squares(0)
    per = groups // chunks

    def hop(i, j):
        c = pl.ds(j * CHUNK, CHUNK)
        return pltpu.make_async_remote_copy(
            src_ref=st_send.at[i, :, c], dst_ref=st_recv.at[i, :, c],
            send_sem=st_ssem.at[i, j], recv_sem=st_rsem.at[i, j],
            device_id=(lax.rem(d + shifts[i], n), t), device_id_type=MESH)

    def send_state(i, j):
        @pl.when(d + shifts[i] < n)
        def _():
            c = pl.ds(j * CHUNK, CHUNK)
            st_send[i, :, c] = state[:, c].astype(BF16)
            hop(i, j).start()

    def take_state(i, j):
        s = shifts[i]

        @pl.when(d >= s)
        def _():
            c = pl.ds(j * CHUNK, CHUNK)
            hop(i, j).wait_recv()
            arrived = st_recv[i, :, c].astype(F32)
            rate = rates[:, c]
            carry[:, c] += jnp.exp(rate * -float(T * (s - 1))) * arrived
            if i + 1 < steps:
                state[:, c] += jnp.exp(rate * -float(T * s)) * arrived

    def inside(j, _):
        c = cols(j)
        y = complex_product(dot(fl[...], v2[:, c]), spec_l[:, c])
        loc[:, c] = dot(gl[...], y) + skip2[:, c] * v2[:, c].astype(F32)
        return 0

    def finish(g, _):
        c = lane(g)
        eight = eights(c)
        terms = first_rows(carry, c)
        for i in range(T // 16):
            r = pl.ds(i * 16, 16)
            rows, terms = next_rows(terms, eight)
            obuf[r, c] = (q2[r, c].astype(F32) * (loc[r, c] + rows)).astype(BF16)
        return 0

    carry[...] = jnp.zeros_like(carry)
    for j in range(chunks):
        lax.fori_loop(j * per, (j + 1) * per, functools.partial(normed, 0), 0)
        c = pl.ds(j * CHUNK, CHUNK)
        state[:, c] += jnp.exp(rates[:, c] * -float(K)) * low[:, c]
        send_state(0, j)
    loads[9].wait()
    gl[...] = gl32[...].astype(BF16)
    loads[10].wait()
    done = 0
    for i in range(steps):
        for j in range(chunks):
            take_state(i, j)
            if i + 1 < steps:
                send_state(i + 1, j)
                continue
            c = pl.ds(j * CHUNK, CHUNK)
            carry[:, c] = carry[:, c] * weight_t[:, c] * jnp.exp(-rates[:, c])
            lax.fori_loop(j * per, (j + 1) * per, finish, 0)
            pltpu.make_async_copy(obuf.at[:, c], lout_h.at[:, c], out_sem.at[j]).start()
        upto = chunks * (i + 1) // max(1, steps - 1)
        if i + 1 < steps:
            lax.fori_loop(done, upto, inside, 0)
            done = upto

    for j in range(chunks):
        @pl.when(d + 1 < n)
        def _(j=j):
            halo(j).wait_send()
    for i, s in enumerate(shifts):
        @pl.when(d + s < n)
        def _(i=i):
            for j in range(chunks):
                hop(i, j).wait_send()
    rout_copy.wait()
    for j in range(chunks):
        c = pl.ds(j * CHUNK, CHUNK)
        pltpu.make_async_copy(obuf.at[:, c], lout_h.at[:, c], out_sem.at[j]).wait()


def on_device(n, tp_n, q1, k1, v1, res, taps, skip1, gain, q2, k2, residues, rates, skip2):
    T, C = q1.shape
    K = taps.shape[0]
    M = residues.shape[0]
    assert T == 2 * K and C % CHUNK == 0
    chunks = C // CHUNK
    steps = (n - 1).bit_length()
    fm, gm = half_bin_tables(2 * K, 2 * K, K, 2 * K)
    fl, gl = half_bin_tables(2 * T, T, 0, T)
    hbm = pl.BlockSpec(memory_space=pl.ANY)
    vmem = pl.BlockSpec(memory_space=pltpu.VMEM)
    wide = pltpu.VMEM((T, C), BF16)
    return pl.pallas_call(
        functools.partial(kernel, n, tp_n),
        out_shape=[jax.ShapeDtypeStruct((T, C), BF16)] * 2,
        in_specs=[hbm] * 5 + [vmem] * 2 + [hbm] * 2 + [vmem] * 3 + [hbm] * 4,
        out_specs=[hbm] * 2,
        scratch_shapes=[
            wide, wide, wide, wide, pltpu.VMEM((K, C), BF16), wide, wide,
            pltpu.VMEM(fm.shape, F32), pltpu.VMEM(gm.shape, F32),
            pltpu.VMEM(fl.shape, F32), pltpu.VMEM(gl.shape, F32),
            pltpu.VMEM(fm.shape, BF16), pltpu.VMEM(gm.shape, BF16),
            pltpu.VMEM(fl.shape, BF16), pltpu.VMEM(gl.shape, BF16),
            pltpu.VMEM((T + K, C), BF16),
            pltpu.VMEM((2 * K, C), F32),
            pltpu.VMEM((2 * T, C), F32),
            wide, wide, wide,
            pltpu.VMEM((T, C), F32),
            wide,
            pltpu.VMEM((K, LANES), F32),
            pltpu.VMEM((2, 8, K), F32),
            pltpu.VMEM((2, tp_n - 1, 8, K), F32),
            pltpu.VMEM((K, LANES), F32),
            pltpu.VMEM((M, C), F32),
            pltpu.VMEM((M, C), F32),
            pltpu.VMEM((8 * M, C), F32),
            pltpu.VMEM((8 * M, C), F32),
            pltpu.VMEM((M, C), F32),
            pltpu.VMEM((M, C), F32),
            pltpu.VMEM((M, C), F32),
            pltpu.VMEM((steps, M, C), BF16),
            pltpu.VMEM((steps, M, C), BF16),
            pltpu.SemaphoreType.DMA((11,)),
            pltpu.SemaphoreType.DMA((chunks + 1,)),
            pltpu.SemaphoreType.DMA((chunks,)),
            pltpu.SemaphoreType.DMA((chunks,)),
            pltpu.SemaphoreType.DMA((2, tp_n - 1)),
            pltpu.SemaphoreType.DMA((2, tp_n - 1)),
            pltpu.SemaphoreType.DMA((steps, chunks)),
            pltpu.SemaphoreType.DMA((steps, chunks)),
        ],
        compiler_params=pltpu.CompilerParams(
            collective_id=0, has_side_effects=True, vmem_limit_bytes=56 * 2**20),
        cost_estimate=pl.CostEstimate(
            flops=2 * 620000 * C, bytes_accessed=10 * T * C * 2, transcendentals=M * C * 16),
    )(q1, k1, v1, res, taps, skip1.reshape(1, C), gain.reshape(1, C), q2, k2, residues, rates,
      skip2.reshape(1, C), jnp.asarray(fm), jnp.asarray(gm), jnp.asarray(fl), jnp.asarray(gl))


def solution(mesh):
    rows = P("ctx", "tp")
    in_specs = (
        rows, rows, rows, rows, P(None, "tp"), P("tp"), P("tp"), rows, rows,
        P(None, "tp"), P(None, "tp"), P("tp"),
    )
    return jax.shard_map(
        functools.partial(on_device, mesh.shape["ctx"], mesh.shape["tp"]),
        mesh=mesh, in_specs=in_specs, out_specs=(rows, rows), check_vma=False)
```

```python
import functools

import jax
import jax.numpy as jnp
import ml_dtypes
import numpy as np
from jax import lax
from jax.experimental import pallas as pl
from jax.experimental.pallas import tpu as pltpu
from jax.sharding import PartitionSpec as P

F32 = jnp.float32
BF16 = jnp.bfloat16
MESH = pl.DeviceIdType.MESH
LANES = 128
CHUNK = 512


def half_bin_tables(period, rows_in, out_from, out_to):
    bins = np.arange(period // 2)[:, None] + 0.5
    angle = 2.0 * np.pi / period * bins * np.arange(period)[None, :]
    forward = np.concatenate([np.cos(angle), -np.sin(angle)], axis=0)[:, :rows_in]
    inverse = np.concatenate([np.cos(angle), -np.sin(angle)], axis=0).T[out_from:out_to] * (2.0 / period)
    return [x.astype(ml_dtypes.bfloat16).astype(np.float32) for x in (forward, inverse)]


def dot(left, right):
    return jnp.dot(left, right, preferred_element_type=F32)


def complex_product(x, h):
    half = x.shape[0] // 2
    xr, xi, hr, hi = x[:half], x[half:], h[:half], h[half:]
    return jnp.concatenate([xr * hr - xi * hi, xr * hi + xi * hr], axis=0).astype(BF16)


def kernel(
    n, tp_n,
    q1_h, k1_h, v1_h, res_h, taps_h, skip1_h, gain_h, q2_h, k2_h, residues_h, rates_h, skip2_h,
    fm_h, gm_h, fl_h, gl_h,
    rout_h, lout_h,
    q1, k1, v1, res, taps, skip1, gain, q2, k2, residues, rates, skip2, fm32, gm32, fl32, gl32, fm, gm, fl, gl,
    buf, spec_m, spec_l, hbuf, rout, v2, loc, obuf,
    sq_acc, sq_send, sq_recv, scale, eight_t, weight_t, up_t, down_t, low, state, carry, st_send, st_recv,
    in_sem, out_sem, halo_send, halo_recv, sq_ssem, sq_rsem, st_ssem, st_rsem,
):
    T, C = q1.shape
    K = taps.shape[0]
    M = residues.shape[0]
    groups = C // LANES
    chunks = C // CHUNK
    steps = (n - 1).bit_length()
    d = lax.axis_index("ctx")
    t = lax.axis_index("tp")

    def lane(g):
        return pl.ds(pl.multiple_of(g * LANES, LANES), LANES)

    def cols(j):
        return pl.ds(j * CHUNK, CHUNK)

    last, top = pl.ds(T - K, K), pl.ds(0, T - K)
    pairs = [
        (k1_h.at[last], k1.at[last]), (v1_h.at[last], v1.at[last]),
        (rates_h, rates), (residues_h, residues), (k1_h.at[top], k1.at[top]), (v1_h.at[top], v1.at[top]),
        (fm_h, fm32), (taps_h, taps), (gm_h, gm32), (skip1_h, skip1), (q1_h, q1), (res_h, res),
        (k2_h, k2), (gain_h, gain), (fl_h, fl32), (gl_h, gl32), (skip2_h, skip2), (q2_h, q2),
    ]
    loads = [pltpu.make_async_copy(a, b, in_sem.at[i]) for i, (a, b) in enumerate(pairs)]
    loads[0].start()
    loads[1].start()

    barrier = pltpu.get_barrier_semaphore()
    shifts = [1 << i for i in range(steps)]
    for s in shifts:
        @pl.when(d + s < n)
        def _(s=s):
            pl.semaphore_signal(barrier, inc=1, device_id=(d + s, t), device_id_type=MESH)

        @pl.when(d >= s)
        def _(s=s):
            pl.semaphore_signal(barrier, inc=1, device_id=(d - s, t), device_id_type=MESH)
    for o in range(1, tp_n):
        pl.semaphore_signal(barrier, inc=1, device_id=(d, lax.rem(t + o, tp_n)), device_id_type=MESH)
    def halo(j):
        c = cols(j)
        return pltpu.make_async_remote_copy(
            src_ref=buf.at[pl.ds(T, K), c], dst_ref=buf.at[pl.ds(0, K), c],
            send_sem=halo_send.at[j], recv_sem=halo_recv.at[j],
            device_id=(lax.rem(d + 1, n), t), device_id_type=MESH)

    def product(row, j):
        c = cols(j)
        r = pl.ds(row, K)
        buf[pl.ds(K + row, K), c] = (k1[r, c].astype(F32) * v1[r, c].astype(F32)).astype(BF16)

    loads[0].wait()
    loads[1].wait()
    for load in loads[2:]:
        load.start()
    for j in range(chunks):
        product(T - K, j)
    peers = tp_n - 1
    for s in shifts:
        peers = peers + (d + s < n).astype(jnp.int32) + (d >= s).astype(jnp.int32)
    pl.semaphore_wait(barrier, peers)
    for j in range(chunks):
        @pl.when(d + 1 < n)
        def _(j=j):
            halo(j).start()
    def medium(row, j):
        c = cols(j)
        r = pl.ds(row, K)
        x = dot(fm[...], buf[pl.ds(row, 2 * K), c])
        filtered = dot(gm[...], complex_product(x, spec_m[:, c]))
        mixed = filtered + skip1[:, c] * buf[pl.ds(K + row, K), c].astype(F32)
        out = (res[r, c].astype(F32) + q1[r, c].astype(F32) * mixed).astype(BF16)
        rout[r, c] = out
        wide = out.astype(F32)
        square = wide * wide
        total = sq_acc[...]
        for i in range(CHUNK // LANES):
            total = total + square[:, i * LANES:(i + 1) * LANES]
        sq_acc[...] = total

    def send_squares(half):
        summed = jnp.sum(sq_acc[...], axis=1, keepdims=True)
        sq_send[half] = jnp.broadcast_to(summed, (K, LANES)).T[:8]
        for o in range(1, tp_n):
            squares(half, o).start()

    def squares(half, o):
        return pltpu.make_async_remote_copy(
            src_ref=sq_send.at[half], dst_ref=sq_recv.at[half, o - 1],
            send_sem=sq_ssem.at[half, o - 1], recv_sem=sq_rsem.at[half, o - 1],
            device_id=(d, lax.rem(t + o, tp_n)), device_id_type=MESH)

    def take_squares(half):
        total = sq_send[half]
        for o in range(1, tp_n):
            squares(half, o).wait()
            total = total + sq_recv[half, o - 1]
        root = lax.rsqrt(total * (1.0 / (C * tp_n)) + 1e-05)
        scale[...] = jnp.concatenate([root] * (K // 8), axis=0).T

    def mode_tables(g, _):
        c = lane(g)
        sub = lax.broadcasted_iota(jnp.int32, (8, LANES), 0).astype(F32)
        rate = rates[:, c]
        eight_t[:, c] = jnp.exp(rate * -8.0)
        weight_t[:, c] = residues[:, c] * jnp.sqrt(rate)
        for m in range(M):
            row = jnp.broadcast_to(rates[pl.ds(m, 1), c], (8, LANES))
            up_t[pl.ds(8 * m, 8), c] = jnp.exp(-row * sub)
            down_t[pl.ds(8 * m, 8), c] = jnp.exp(-row * (7.0 - sub))
        return 0

    def eights(c):
        return [jnp.broadcast_to(eight_t[pl.ds(m, 1), c], (8, LANES)) for m in range(M)]

    def first_rows(factor, c):
        return [up_t[pl.ds(8 * m, 8), c] * factor[pl.ds(m, 1), c] for m in range(M)]

    def tree_sum(terms):
        while len(terms) > 1:
            terms = [a + b for a, b in zip(terms[::2], terms[1::2])] + terms[len(terms) // 2 * 2:]
        return terms[0]

    def next_rows(terms, eight):
        top = tree_sum(terms)
        terms = [p * a for p, a in zip(terms, eight)]
        bottom = tree_sum(terms)
        return jnp.concatenate([top, bottom], axis=0), [p * a for p, a in zip(terms, eight)]

    def normed(half, g, _):
        c = lane(g)
        eight = eights(c)
        held = [jnp.zeros((8, LANES), F32)] * M
        for i in range(K // 16):
            r = pl.ds(half * K + i * 16, 16)
            value = (k2[r, c].astype(F32) * rout[r, c].astype(F32) * scale[pl.ds(i * 16, 16), :] * gain[:, c]).astype(BF16)
            v2[r, c] = value
            wide = value.astype(F32)
            held = [h * a + wide[:8] for h, a in zip(held, eight)]
            held = [h * a + wide[8:] for h, a in zip(held, eight)]
        into = low if half == 0 else state
        for m in range(M):
            into[pl.ds(m, 1), c] = jnp.sum(held[m] * down_t[pl.ds(8 * m, 8), c], axis=0, keepdims=True)
        return 0

    def long_taps(g, _):
        c = lane(g)
        eight = eights(c)
        terms = first_rows(weight_t, c)
        for i in range(T // 16):
            rows, terms = next_rows(terms, eight)
            hbuf[pl.ds(i * 16, 16), c] = rows.astype(BF16)
        return 0

    def long_spectrum(j):
        spec_l[:, cols(j)] = dot(fl[...], hbuf[:, cols(j)])

    loads[2].wait()
    loads[3].wait()
    lax.fori_loop(0, groups, mode_tables, 0)

    @pl.when(d == 0)
    def _():
        buf[pl.ds(0, K), :] = jnp.zeros((K, C), BF16)

    for i in range(4, 12):
        loads[i].wait()
    fm[...] = fm32[...].astype(BF16)
    gm[...] = gm32[...].astype(BF16)
    for j in range(chunks):
        product(0, j)
    sq_acc[...] = jnp.zeros_like(sq_acc)
    for j in range(chunks):
        spec_m[:, cols(j)] = dot(fm[:, :K], taps[:, cols(j)])
        medium(K, j)
    send_squares(1)
    lax.fori_loop(0, groups, long_taps, 0)
    for i in range(12, 18):
        loads[i].wait()
    fl[...] = fl32[...].astype(BF16)
    gl[...] = gl32[...].astype(BF16)
    take_squares(1)
    lax.fori_loop(0, groups, functools.partial(normed, 1), 0)

    sq_acc[...] = jnp.zeros_like(sq_acc)
    for j in range(chunks):
        @pl.when(d >= 1)
        def _(j=j):
            halo(j).wait_recv()
        medium(0, j)
    send_squares(0)
    rout_copy = pltpu.make_async_copy(rout, rout_h, out_sem.at[chunks])
    rout_copy.start()
    for j in range(chunks):
        long_spectrum(j)
    take_squares(0)

    per = groups // chunks

    def hop(i, j):
        c = cols(j)
        return pltpu.make_async_remote_copy(
            src_ref=st_send.at[i, :, c], dst_ref=st_recv.at[i, :, c],
            send_sem=st_ssem.at[i, j], recv_sem=st_rsem.at[i, j],
            device_id=(lax.rem(d + shifts[i], n), t), device_id_type=MESH)

    def send_state(i, j):
        @pl.when(d + shifts[i] < n)
        def _():
            c = cols(j)
            st_send[i, :, c] = state[:, c].astype(BF16)
            hop(i, j).start()

    def take_state(i, j):
        s = shifts[i]

        @pl.when(d >= s)
        def _():
            c = cols(j)
            hop(i, j).wait_recv()
            arrived = st_recv[i, :, c].astype(F32)
            rate = rates[:, c]
            carry[:, c] += jnp.exp(rate * -float(T * (s - 1))) * arrived
            if i + 1 < steps:
                state[:, c] += jnp.exp(rate * -float(T * s)) * arrived

    def inside(j):
        c = cols(j)
        y = complex_product(dot(fl[...], v2[:, c]), spec_l[:, c])
        loc[:, c] = dot(gl[...], y) + skip2[:, c] * v2[:, c].astype(F32)

    def finish(g, _):
        c = lane(g)
        eight = eights(c)
        terms = first_rows(carry, c)
        for i in range(T // 16):
            r = pl.ds(i * 16, 16)
            rows, terms = next_rows(terms, eight)
            obuf[r, c] = (q2[r, c].astype(F32) * (loc[r, c] + rows)).astype(BF16)
        return 0

    carry[...] = jnp.zeros_like(carry)
    for j in range(chunks):
        lax.fori_loop(j * per, (j + 1) * per, functools.partial(normed, 0), 0)
        c = cols(j)
        state[:, c] += jnp.exp(rates[:, c] * -float(K)) * low[:, c]
        send_state(0, j)
    waiting = list(range(chunks))
    for i in range(steps - 1):
        for j in range(chunks):
            if j % 2 == 0 and waiting:
                inside(waiting.pop(0))
            take_state(i, j)
            send_state(i + 1, j)
    for j in waiting:
        inside(j)
    for j in range(chunks):
        c = cols(j)
        take_state(steps - 1, j)
        carry[:, c] = carry[:, c] * weight_t[:, c] * jnp.exp(-rates[:, c])
        lax.fori_loop(j * per, (j + 1) * per, finish, 0)
        pltpu.make_async_copy(obuf.at[:, c], lout_h.at[:, c], out_sem.at[j]).start()

    for j in range(chunks):
        @pl.when(d + 1 < n)
        def _(j=j):
            halo(j).wait_send()
    for i, s in enumerate(shifts):
        @pl.when(d + s < n)
        def _(i=i):
            for j in range(chunks):
                hop(i, j).wait_send()
    rout_copy.wait()
    for j in range(chunks):
        c = cols(j)
        pltpu.make_async_copy(obuf.at[:, c], lout_h.at[:, c], out_sem.at[j]).wait()


def on_device(n, tp_n, q1, k1, v1, res, taps, skip1, gain, q2, k2, residues, rates, skip2):
    T, C = q1.shape
    K = taps.shape[0]
    M = residues.shape[0]
    assert T == 2 * K and C % CHUNK == 0
    chunks = C // CHUNK
    steps = (n - 1).bit_length()
    fm, gm = half_bin_tables(2 * K, 2 * K, K, 2 * K)
    fl, gl = half_bin_tables(2 * T, T, 0, T)
    hbm = pl.BlockSpec(memory_space=pl.ANY)
    line = pltpu.VMEM((1, C), F32)
    modes = pltpu.VMEM((M, C), F32)
    wide = pltpu.VMEM((T, C), BF16)
    return pl.pallas_call(
        functools.partial(kernel, n, tp_n),
        out_shape=[jax.ShapeDtypeStruct((T, C), BF16)] * 2,
        in_specs=[hbm] * 16,
        out_specs=[hbm] * 2,
        scratch_shapes=[
            wide, wide, wide, wide, pltpu.VMEM((K, C), BF16), line, line, wide, wide,
            modes, modes, line,
            pltpu.VMEM(fm.shape, F32), pltpu.VMEM(gm.shape, F32),
            pltpu.VMEM(fl.shape, F32), pltpu.VMEM(gl.shape, F32),
            pltpu.VMEM(fm.shape, BF16), pltpu.VMEM(gm.shape, BF16),
            pltpu.VMEM(fl.shape, BF16), pltpu.VMEM(gl.shape, BF16),
            pltpu.VMEM((T + K, C), BF16),
            pltpu.VMEM((2 * K, C), F32),
            pltpu.VMEM((2 * T, C), F32),
            wide, wide, wide,
            pltpu.VMEM((T, C), F32),
            wide,
            pltpu.VMEM((K, LANES), F32),
            pltpu.VMEM((2, 8, K), F32),
            pltpu.VMEM((2, tp_n - 1, 8, K), F32),
            pltpu.VMEM((K, LANES), F32),
            modes,
            modes,
            pltpu.VMEM((8 * M, C), F32),
            pltpu.VMEM((8 * M, C), F32),
            modes,
            modes,
            modes,
            pltpu.VMEM((steps, M, C), BF16),
            pltpu.VMEM((steps, M, C), BF16),
            pltpu.SemaphoreType.DMA((18,)),
            pltpu.SemaphoreType.DMA((chunks + 1,)),
            pltpu.SemaphoreType.DMA((chunks,)),
            pltpu.SemaphoreType.DMA((chunks,)),
            pltpu.SemaphoreType.DMA((2, tp_n - 1)),
            pltpu.SemaphoreType.DMA((2, tp_n - 1)),
            pltpu.SemaphoreType.DMA((steps, chunks)),
            pltpu.SemaphoreType.DMA((steps, chunks)),
        ],
        compiler_params=pltpu.CompilerParams(
            collective_id=0, has_side_effects=True, vmem_limit_bytes=56 * 2**20),
        cost_estimate=pl.CostEstimate(
            flops=2 * 620000 * C, bytes_accessed=10 * T * C * 2, transcendentals=M * C * 16),
    )(q1, k1, v1, res, taps, skip1.reshape(1, C), gain.reshape(1, C), q2, k2, residues, rates,
      skip2.reshape(1, C), jnp.asarray(fm), jnp.asarray(gm), jnp.asarray(fl), jnp.asarray(gl))


def solution(mesh):
    rows = P("ctx", "tp")
    in_specs = (
        rows, rows, rows, rows, P(None, "tp"), P("tp"), P("tp"), rows, rows,
        P(None, "tp"), P(None, "tp"), P("tp"),
    )
    return jax.shard_map(
        functools.partial(on_device, mesh.shape["ctx"], mesh.shape["tp"]),
        mesh=mesh, in_specs=in_specs, out_specs=(rows, rows), check_vma=False)
```

```python
import functools

import jax
import jax.numpy as jnp
import ml_dtypes
import numpy as np
from jax import lax
from jax.experimental import pallas as pl
from jax.experimental.pallas import tpu as pltpu
from jax.sharding import PartitionSpec as P

F32 = jnp.float32
BF16 = jnp.bfloat16
MESH = pl.DeviceIdType.MESH
LANES = 128
CHUNK = 512


def half_bin_tables(period, rows_in, out_from, out_to):
    bins = np.arange(period // 2)[:, None] + 0.5
    angle = 2.0 * np.pi / period * bins * np.arange(period)[None, :]
    forward = np.concatenate([np.cos(angle), -np.sin(angle)], axis=0)[:, :rows_in]
    inverse = np.concatenate([np.cos(angle), -np.sin(angle)], axis=0).T[out_from:out_to] * (2.0 / period)
    return [x.astype(ml_dtypes.bfloat16).astype(np.float32) for x in (forward, inverse)]


def dot(left, right):
    return jnp.dot(left, right, preferred_element_type=F32)


def complex_product(x, h):
    half = x.shape[0] // 2
    xr, xi, hr, hi = x[:half], x[half:], h[:half], h[half:]
    return jnp.concatenate([xr * hr - xi * hi, xr * hi + xi * hr], axis=0).astype(BF16)


def kernel(
    n, tp_n,
    q1_h, k1_h, v1_h, res_h, taps_h, skip1_h, gain_h, q2_h, k2_h, residues_h, rates_h, skip2_h,
    fm_h, gm_h, fl_h, gl_h,
    rout_h, lout_h,
    q1, k1, v1, res, taps, skip1, gain, q2, k2, residues, rates, skip2, fm32, gm32, fl32, gl32, fm, gm, fl, gl,
    buf, spec_m, spec_l, hbuf, rout, v2, loc, obuf,
    sq_acc, sq_send, sq_recv, scale, eight_t, weight_t, later_t, up_t, down_t, low, state, carry, st_send, st_recv,
    in_sem, out_sem, halo_send, halo_recv, sq_ssem, sq_rsem, st_ssem, st_rsem,
):
    T, C = q1.shape
    K = taps.shape[0]
    M = residues.shape[0]
    groups = C // LANES
    chunks = C // CHUNK
    steps = (n - 1).bit_length()
    d = lax.axis_index("ctx")
    t = lax.axis_index("tp")

    def lane(g):
        return pl.ds(pl.multiple_of(g * LANES, LANES), LANES)

    def cols(j):
        return pl.ds(j * CHUNK, CHUNK)

    last, top = pl.ds(T - K, K), pl.ds(0, T - K)
    pairs = [
        (k1_h.at[last], k1.at[last]), (v1_h.at[last], v1.at[last]),
        (rates_h, rates), (residues_h, residues), (k1_h.at[top], k1.at[top]), (v1_h.at[top], v1.at[top]),
        (fm_h, fm32), (taps_h, taps), (gm_h, gm32), (skip1_h, skip1), (q1_h, q1), (res_h, res),
        (k2_h, k2), (gain_h, gain), (fl_h, fl32), (gl_h, gl32), (skip2_h, skip2), (q2_h, q2),
    ]
    loads = [pltpu.make_async_copy(a, b, in_sem.at[i]) for i, (a, b) in enumerate(pairs)]
    loads[0].start()
    loads[1].start()

    barrier = pltpu.get_barrier_semaphore()
    shifts = [1 << i for i in range(steps)]
    for s in shifts:
        @pl.when(d + s < n)
        def _(s=s):
            pl.semaphore_signal(barrier, inc=1, device_id=(d + s, t), device_id_type=MESH)

        @pl.when(d >= s)
        def _(s=s):
            pl.semaphore_signal(barrier, inc=1, device_id=(d - s, t), device_id_type=MESH)
    for o in range(1, tp_n):
        pl.semaphore_signal(barrier, inc=1, device_id=(d, lax.rem(t + o, tp_n)), device_id_type=MESH)
    def halo(j):
        c = cols(j)
        return pltpu.make_async_remote_copy(
            src_ref=buf.at[pl.ds(T, K), c], dst_ref=buf.at[pl.ds(0, K), c],
            send_sem=halo_send.at[j], recv_sem=halo_recv.at[j],
            device_id=(lax.rem(d + 1, n), t), device_id_type=MESH)

    def product(row, j):
        c = cols(j)
        r = pl.ds(row, K)
        buf[pl.ds(K + row, K), c] = (k1[r, c].astype(F32) * v1[r, c].astype(F32)).astype(BF16)

    loads[0].wait()
    loads[1].wait()
    for load in loads[2:]:
        load.start()
    for j in range(chunks):
        product(T - K, j)
    peers = tp_n - 1
    for s in shifts:
        peers = peers + (d + s < n).astype(jnp.int32) + (d >= s).astype(jnp.int32)
    pl.semaphore_wait(barrier, peers)
    for j in range(chunks):
        @pl.when(d + 1 < n)
        def _(j=j):
            halo(j).start()
    def medium(row, j):
        c = cols(j)
        r = pl.ds(row, K)
        x = dot(fm[...], buf[pl.ds(row, 2 * K), c])
        filtered = dot(gm[...], complex_product(x, spec_m[:, c]))
        mixed = filtered + skip1[:, c] * buf[pl.ds(K + row, K), c].astype(F32)
        out = (res[r, c].astype(F32) + q1[r, c].astype(F32) * mixed).astype(BF16)
        rout[r, c] = out
        wide = out.astype(F32)
        square = wide * wide
        total = sq_acc[...]
        for i in range(CHUNK // LANES):
            total = total + square[:, i * LANES:(i + 1) * LANES]
        sq_acc[...] = total

    def send_squares(half):
        summed = jnp.sum(sq_acc[...].T, axis=0, keepdims=True)
        sq_send[half] = jnp.broadcast_to(summed, (8, K))
        for o in range(1, tp_n):
            squares(half, o).start()

    def squares(half, o):
        return pltpu.make_async_remote_copy(
            src_ref=sq_send.at[half], dst_ref=sq_recv.at[half, o - 1],
            send_sem=sq_ssem.at[half, o - 1], recv_sem=sq_rsem.at[half, o - 1],
            device_id=(d, lax.rem(t + o, tp_n)), device_id_type=MESH)

    def take_squares(half):
        total = sq_send[half]
        for o in range(1, tp_n):
            squares(half, o).wait()
            total = total + sq_recv[half, o - 1]
        root = lax.rsqrt(total * (1.0 / (C * tp_n)) + 1e-05)
        scale[...] = jnp.concatenate([root] * (K // 8), axis=0).T

    def mode_tables(g, _):
        c = lane(g)
        sub = lax.broadcasted_iota(jnp.int32, (8, LANES), 0).astype(F32)
        rate = rates[:, c]
        eight_t[:, c] = jnp.exp(rate * -8.0)
        weight_t[:, c] = residues[:, c] * jnp.sqrt(rate)
        later_t[:, c] = weight_t[:, c] * jnp.exp(-rate)
        for m in range(M):
            row = jnp.broadcast_to(rates[pl.ds(m, 1), c], (8, LANES))
            up_t[pl.ds(8 * m, 8), c] = jnp.exp(-row * sub)
            down_t[pl.ds(8 * m, 8), c] = jnp.exp(-row * (7.0 - sub))
        return 0

    def eights(c):
        return [jnp.broadcast_to(eight_t[pl.ds(m, 1), c], (8, LANES)) for m in range(M)]

    def first_rows(factor, c):
        return [up_t[pl.ds(8 * m, 8), c] * factor[pl.ds(m, 1), c] for m in range(M)]

    def tree_sum(terms):
        while len(terms) > 1:
            terms = [a + b for a, b in zip(terms[::2], terms[1::2])] + terms[len(terms) // 2 * 2:]
        return terms[0]

    def next_rows(terms, eight):
        top = tree_sum(terms)
        terms = [p * a for p, a in zip(terms, eight)]
        bottom = tree_sum(terms)
        return jnp.concatenate([top, bottom], axis=0), [p * a for p, a in zip(terms, eight)]

    def normed(half, g, _):
        c = lane(g)
        eight = eights(c)
        held = [jnp.zeros((8, LANES), F32)] * M
        for i in range(K // 16):
            r = pl.ds(half * K + i * 16, 16)
            value = (k2[r, c].astype(F32) * rout[r, c].astype(F32) * scale[pl.ds(i * 16, 16), :] * gain[:, c]).astype(BF16)
            v2[r, c] = value
            wide = value.astype(F32)
            held = [h * a + wide[:8] for h, a in zip(held, eight)]
            held = [h * a + wide[8:] for h, a in zip(held, eight)]
        into = low if half == 0 else state
        for m in range(M):
            into[pl.ds(m, 1), c] = jnp.sum(held[m] * down_t[pl.ds(8 * m, 8), c], axis=0, keepdims=True)
        return 0

    def long_taps(g, _):
        c = lane(g)
        eight = eights(c)
        terms = first_rows(weight_t, c)
        for i in range(T // 16):
            rows, terms = next_rows(terms, eight)
            hbuf[pl.ds(i * 16, 16), c] = rows.astype(BF16)
        return 0

    def long_spectrum(j):
        spec_l[:, cols(j)] = dot(fl[...], hbuf[:, cols(j)])

    loads[2].wait()
    loads[3].wait()
    lax.fori_loop(0, groups, mode_tables, 0)

    @pl.when(d == 0)
    def _():
        buf[pl.ds(0, K), :] = jnp.zeros((K, C), BF16)

    for i in range(4, 12):
        loads[i].wait()
    fm[...] = fm32[...].astype(BF16)
    gm[...] = gm32[...].astype(BF16)
    for j in range(chunks):
        product(0, j)
    sq_acc[...] = jnp.zeros_like(sq_acc)
    for j in range(chunks):
        spec_m[:, cols(j)] = dot(fm[:, :K], taps[:, cols(j)])
        medium(K, j)
    send_squares(1)
    lax.fori_loop(0, groups, long_taps, 0)
    for i in range(12, 18):
        loads[i].wait()
    fl[...] = fl32[...].astype(BF16)
    gl[...] = gl32[...].astype(BF16)
    take_squares(1)
    lax.fori_loop(0, groups, functools.partial(normed, 1), 0)

    sq_acc[...] = jnp.zeros_like(sq_acc)
    for j in range(chunks):
        @pl.when(d >= 1)
        def _(j=j):
            halo(j).wait_recv()
        medium(0, j)
    send_squares(0)
    rout_copy = pltpu.make_async_copy(rout, rout_h, out_sem.at[chunks])
    rout_copy.start()
    for j in range(chunks):
        long_spectrum(j)
    take_squares(0)

    per = groups // chunks

    def hop(i, j):
        c = cols(j)
        return pltpu.make_async_remote_copy(
            src_ref=st_send.at[i, :, c], dst_ref=st_recv.at[i, :, c],
            send_sem=st_ssem.at[i, j], recv_sem=st_rsem.at[i, j],
            device_id=(lax.rem(d + shifts[i], n), t), device_id_type=MESH)

    def send_state(i, j):
        @pl.when(d + shifts[i] < n)
        def _():
            c = cols(j)
            st_send[i, :, c] = state[:, c].astype(BF16)
            hop(i, j).start()

    def take_state(i, j):
        s = shifts[i]

        @pl.when(d >= s)
        def _():
            c = cols(j)
            rate = rates[:, c]
            near, far = jnp.exp(rate * -float(T * (s - 1))), jnp.exp(rate * -float(T * s))
            hop(i, j).wait_recv()
            arrived = st_recv[i, :, c].astype(F32)
            carry[:, c] += near * arrived
            if i + 1 < steps:
                state[:, c] += far * arrived

    def inside(j):
        c = cols(j)
        y = complex_product(dot(fl[...], v2[:, c]), spec_l[:, c])
        loc[:, c] = dot(gl[...], y) + skip2[:, c] * v2[:, c].astype(F32)

    def finish(g, _):
        c = lane(g)
        eight = eights(c)
        terms = first_rows(carry, c)
        for i in range(T // 16):
            r = pl.ds(i * 16, 16)
            rows, terms = next_rows(terms, eight)
            obuf[r, c] = (q2[r, c].astype(F32) * (loc[r, c] + rows)).astype(BF16)
        return 0

    carry[...] = jnp.zeros_like(carry)
    for j in range(chunks):
        lax.fori_loop(j * per, (j + 1) * per, functools.partial(normed, 0), 0)
        c = cols(j)
        state[:, c] += jnp.exp(rates[:, c] * -float(K)) * low[:, c]
        send_state(0, j)
    waiting = list(range(chunks))
    for i in range(steps - 1):
        for j in range(chunks):
            if j % 2 == 0 and waiting:
                inside(waiting.pop(0))
            take_state(i, j)
            send_state(i + 1, j)
    for j in waiting:
        inside(j)
    for j in range(chunks):
        c = cols(j)
        take_state(steps - 1, j)
        carry[:, c] = carry[:, c] * later_t[:, c]
        lax.fori_loop(j * per, (j + 1) * per, finish, 0)
        pltpu.make_async_copy(obuf.at[:, c], lout_h.at[:, c], out_sem.at[j]).start()

    for j in range(chunks):
        @pl.when(d + 1 < n)
        def _(j=j):
            halo(j).wait_send()
    for i, s in enumerate(shifts):
        @pl.when(d + s < n)
        def _(i=i):
            for j in range(chunks):
                hop(i, j).wait_send()
    rout_copy.wait()
    for j in range(chunks):
        c = cols(j)
        pltpu.make_async_copy(obuf.at[:, c], lout_h.at[:, c], out_sem.at[j]).wait()


def hand_on(a_from, b_from, a_to, b_to, sem):
    pieces = sem.shape[1]
    rows = a_from.shape[0] // pieces
    copies = [
        pltpu.make_async_copy(x.at[pl.ds(i * rows, rows)], y.at[pl.ds(i * rows, rows)], sem.at[k, i])
        for k, (x, y) in enumerate([(a_from, a_to), (b_from, b_to)]) for i in range(pieces)
    ]
    for copy in copies:
        copy.start()
    for copy in copies:
        copy.wait()


def on_device(n, tp_n, q1, k1, v1, res, taps, skip1, gain, q2, k2, residues, rates, skip2):
    T, C = q1.shape
    K = taps.shape[0]
    M = residues.shape[0]
    assert T == 2 * K and C % CHUNK == 0
    chunks = C // CHUNK
    steps = (n - 1).bit_length()
    fm, gm = half_bin_tables(2 * K, 2 * K, K, 2 * K)
    fl, gl = half_bin_tables(2 * T, T, 0, T)
    hbm = pl.BlockSpec(memory_space=pl.ANY)
    line = pltpu.VMEM((1, C), F32)
    modes = pltpu.VMEM((M, C), F32)
    wide = pltpu.VMEM((T, C), BF16)
    outs = pl.pallas_call(
        functools.partial(kernel, n, tp_n),
        out_shape=[jax.ShapeDtypeStruct((T, C), BF16)] * 2,
        in_specs=[hbm] * 16,
        out_specs=[hbm] * 2,
        scratch_shapes=[
            wide, wide, wide, wide, pltpu.VMEM((K, C), BF16), line, line, wide, wide,
            modes, modes, line,
            pltpu.VMEM(fm.shape, F32), pltpu.VMEM(gm.shape, F32),
            pltpu.VMEM(fl.shape, F32), pltpu.VMEM(gl.shape, F32),
            pltpu.VMEM(fm.shape, BF16), pltpu.VMEM(gm.shape, BF16),
            pltpu.VMEM(fl.shape, BF16), pltpu.VMEM(gl.shape, BF16),
            pltpu.VMEM((T + K, C), BF16),
            pltpu.VMEM((2 * K, C), F32),
            pltpu.VMEM((2 * T, C), F32),
            wide, wide, wide,
            pltpu.VMEM((T, C), F32),
            wide,
            pltpu.VMEM((K, LANES), F32),
            pltpu.VMEM((2, 8, K), F32),
            pltpu.VMEM((2, tp_n - 1, 8, K), F32),
            pltpu.VMEM((K, LANES), F32),
            modes,
            modes,
            modes,
            pltpu.VMEM((8 * M, C), F32),
            pltpu.VMEM((8 * M, C), F32),
            modes,
            modes,
            modes,
            pltpu.VMEM((steps, M, C), BF16),
            pltpu.VMEM((steps, M, C), BF16),
            pltpu.SemaphoreType.DMA((18,)),
            pltpu.SemaphoreType.DMA((chunks + 1,)),
            pltpu.SemaphoreType.DMA((chunks,)),
            pltpu.SemaphoreType.DMA((chunks,)),
            pltpu.SemaphoreType.DMA((2, tp_n - 1)),
            pltpu.SemaphoreType.DMA((2, tp_n - 1)),
            pltpu.SemaphoreType.DMA((steps, chunks)),
            pltpu.SemaphoreType.DMA((steps, chunks)),
        ],
        compiler_params=pltpu.CompilerParams(
            collective_id=0, has_side_effects=True, vmem_limit_bytes=56 * 2**20),
        cost_estimate=pl.CostEstimate(
            flops=2 * 620000 * C, bytes_accessed=10 * T * C * 2, transcendentals=M * C * 16),
    )(q1, k1, v1, res, taps, skip1.reshape(1, C), gain.reshape(1, C), q2, k2, residues, rates,
      skip2.reshape(1, C), jnp.asarray(fm), jnp.asarray(gm), jnp.asarray(fl), jnp.asarray(gl))
    plain = pl.BlockSpec(memory_space=pltpu.HBM)
    return pl.pallas_call(
        hand_on,
        out_shape=[jax.ShapeDtypeStruct((T, C), BF16)] * 2,
        in_specs=[plain] * 2,
        out_specs=[plain] * 2,
        scratch_shapes=[pltpu.SemaphoreType.DMA((2, 8))],
        cost_estimate=pl.CostEstimate(flops=0, bytes_accessed=8 * T * C, transcendentals=0),
    )(*outs)


def solution(mesh):
    rows = P("ctx", "tp")
    in_specs = (
        rows, rows, rows, rows, P(None, "tp"), P("tp"), P("tp"), rows, rows,
        P(None, "tp"), P(None, "tp"), P("tp"),
    )
    return jax.shard_map(
        functools.partial(on_device, mesh.shape["ctx"], mesh.shape["tp"]),
        mesh=mesh, in_specs=in_specs, out_specs=(rows, rows), check_vma=False)
```

```python
import functools

import jax
import jax.numpy as jnp
import ml_dtypes
import numpy as np
from jax import lax
from jax.experimental import pallas as pl
from jax.experimental.pallas import tpu as pltpu
from jax.sharding import PartitionSpec as P

F32 = jnp.float32
BF16 = jnp.bfloat16
MESH = pl.DeviceIdType.MESH
LANES = 128
CHUNK = 512


def half_bin_tables(period, rows_in, out_from, out_to):
    bins = np.arange(period // 2)[:, None] + 0.5
    angle = 2.0 * np.pi / period * bins * np.arange(period)[None, :]
    forward = np.concatenate([np.cos(angle), -np.sin(angle)], axis=0)[:, :rows_in]
    inverse = np.concatenate([np.cos(angle), -np.sin(angle)], axis=0).T[out_from:out_to] * (2.0 / period)
    return [x.astype(ml_dtypes.bfloat16).astype(np.float32) for x in (forward, inverse)]


def dot(left, right):
    return jnp.dot(left, right, preferred_element_type=F32)


def complex_product(x, h):
    half = x.shape[0] // 2
    xr, xi, hr, hi = x[:half], x[half:], h[:half], h[half:]
    return jnp.concatenate([xr * hr - xi * hi, xr * hi + xi * hr], axis=0).astype(BF16)


def kernel(
    n, tp_n,
    q1_h, k1_h, v1_h, res_h, taps_h, skip1_h, gain_h, q2_h, k2_h, residues_h, rates_h, skip2_h,
    fm_h, gm_h, fl_h, gl_h,
    rout_h, lout_h,
    q1, k1, v1, res, taps, skip1, gain, q2, k2, residues, rates, skip2, fm32, gm32, fl32, gl32, fm, gm, fl, gl,
    buf, spec_m, spec_l, hbuf, rout, v2, loc, obuf,
    sq_acc, sq_send, sq_recv, scale, eight_t, weight_t, later_t, up_t, down_t, low, state, carry, st_send, st_recv,
    in_sem, out_sem, halo_send, halo_recv, sq_ssem, sq_rsem, st_ssem, st_rsem,
):
    T, C = q1.shape
    K = taps.shape[0]
    M = residues.shape[0]
    groups = C // LANES
    chunks = C // CHUNK
    steps = (n - 1).bit_length()
    d = lax.axis_index("ctx")
    t = lax.axis_index("tp")

    def lane(g):
        return pl.ds(pl.multiple_of(g * LANES, LANES), LANES)

    def cols(j):
        return pl.ds(j * CHUNK, CHUNK)

    last, top = pl.ds(T - K, K), pl.ds(0, T - K)
    pairs = [
        (k1_h.at[last], k1.at[last]), (v1_h.at[last], v1.at[last]),
        (rates_h, rates), (residues_h, residues), (k1_h.at[top], k1.at[top]), (v1_h.at[top], v1.at[top]),
        (fm_h, fm32), (taps_h, taps), (gm_h, gm32), (skip1_h, skip1), (q1_h, q1), (res_h, res),
        (k2_h, k2), (gain_h, gain), (fl_h, fl32), (gl_h, gl32), (skip2_h, skip2), (q2_h, q2),
    ]
    loads = [pltpu.make_async_copy(a, b, in_sem.at[i]) for i, (a, b) in enumerate(pairs)]
    loads[0].start()
    loads[1].start()

    barrier = pltpu.get_barrier_semaphore()
    shifts = [1 << i for i in range(steps)]
    for s in shifts:
        @pl.when(d + s < n)
        def _(s=s):
            pl.semaphore_signal(barrier, inc=1, device_id=(d + s, t), device_id_type=MESH)

        @pl.when(d >= s)
        def _(s=s):
            pl.semaphore_signal(barrier, inc=1, device_id=(d - s, t), device_id_type=MESH)
    for o in range(1, tp_n):
        pl.semaphore_signal(barrier, inc=1, device_id=(d, lax.rem(t + o, tp_n)), device_id_type=MESH)
    def halo(j):
        c = cols(j)
        return pltpu.make_async_remote_copy(
            src_ref=buf.at[pl.ds(T, K), c], dst_ref=buf.at[pl.ds(0, K), c],
            send_sem=halo_send.at[j], recv_sem=halo_recv.at[j],
            device_id=(lax.rem(d + 1, n), t), device_id_type=MESH)

    def product(row, j):
        c = cols(j)
        r = pl.ds(row, K)
        buf[pl.ds(K + row, K), c] = (k1[r, c].astype(F32) * v1[r, c].astype(F32)).astype(BF16)

    loads[0].wait()
    loads[1].wait()
    for load in loads[2:]:
        load.start()
    for j in range(chunks):
        product(T - K, j)
    peers = tp_n - 1
    for s in shifts:
        peers = peers + (d + s < n).astype(jnp.int32) + (d >= s).astype(jnp.int32)
    pl.semaphore_wait(barrier, peers)
    for j in range(chunks):
        @pl.when(d + 1 < n)
        def _(j=j):
            halo(j).start()
    def medium(row, j):
        c = cols(j)
        r = pl.ds(row, K)
        x = dot(fm[...], buf[pl.ds(row, 2 * K), c])
        filtered = dot(gm[...], complex_product(x, spec_m[:, c]))
        mixed = filtered + skip1[:, c] * buf[pl.ds(K + row, K), c].astype(F32)
        out = (res[r, c].astype(F32) + q1[r, c].astype(F32) * mixed).astype(BF16)
        rout[r, c] = out
        wide = out.astype(F32)
        square = wide * wide
        total = sq_acc[...]
        for i in range(CHUNK // LANES):
            total = total + square[:, i * LANES:(i + 1) * LANES]
        sq_acc[...] = total

    def send_squares(half):
        summed = jnp.sum(sq_acc[...].T, axis=0, keepdims=True)
        sq_send[half] = jnp.broadcast_to(summed, (8, K))
        for o in range(1, tp_n):
            squares(half, o).start()

    def squares(half, o):
        return pltpu.make_async_remote_copy(
            src_ref=sq_send.at[half], dst_ref=sq_recv.at[half, o - 1],
            send_sem=sq_ssem.at[half, o - 1], recv_sem=sq_rsem.at[half, o - 1],
            device_id=(d, lax.rem(t + o, tp_n)), device_id_type=MESH)

    def take_squares(half):
        total = sq_send[half]
        for o in range(1, tp_n):
            squares(half, o).wait()
            total = total + sq_recv[half, o - 1]
        root = lax.rsqrt(total * (1.0 / (C * tp_n)) + 1e-05)
        scale[...] = jnp.concatenate([root] * (K // 8), axis=0).T

    def mode_tables(g, _):
        c = lane(g)
        sub = lax.broadcasted_iota(jnp.int32, (8, LANES), 0).astype(F32)
        rate = rates[:, c]
        eight_t[:, c] = jnp.exp(rate * -8.0)
        weight_t[:, c] = residues[:, c] * jnp.sqrt(rate)
        later_t[:, c] = weight_t[:, c] * jnp.exp(-rate)
        for m in range(M):
            row = jnp.broadcast_to(rates[pl.ds(m, 1), c], (8, LANES))
            up_t[pl.ds(8 * m, 8), c] = jnp.exp(-row * sub)
            down_t[pl.ds(8 * m, 8), c] = jnp.exp(-row * (7.0 - sub))
        return 0

    def eights(c):
        return [jnp.broadcast_to(eight_t[pl.ds(m, 1), c], (8, LANES)) for m in range(M)]

    def first_rows(factor, c):
        return [up_t[pl.ds(8 * m, 8), c] * factor[pl.ds(m, 1), c] for m in range(M)]

    def tree_sum(terms):
        while len(terms) > 1:
            terms = [a + b for a, b in zip(terms[::2], terms[1::2])] + terms[len(terms) // 2 * 2:]
        return terms[0]

    def next_rows(terms, eight):
        top = tree_sum(terms)
        terms = [p * a for p, a in zip(terms, eight)]
        bottom = tree_sum(terms)
        return jnp.concatenate([top, bottom], axis=0), [p * a for p, a in zip(terms, eight)]

    def normed(half, g, _):
        c = lane(g)
        eight = eights(c)
        held = [jnp.zeros((8, LANES), F32)] * M
        for i in range(K // 16):
            r = pl.ds(half * K + i * 16, 16)
            value = (k2[r, c].astype(F32) * rout[r, c].astype(F32) * scale[pl.ds(i * 16, 16), :] * gain[:, c]).astype(BF16)
            v2[r, c] = value
            wide = value.astype(F32)
            held = [h * a + wide[:8] for h, a in zip(held, eight)]
            held = [h * a + wide[8:] for h, a in zip(held, eight)]
        into = low if half == 0 else state
        for m in range(M):
            into[pl.ds(m, 1), c] = jnp.sum(held[m] * down_t[pl.ds(8 * m, 8), c], axis=0, keepdims=True)
        return 0

    def long_taps(g, _):
        c = lane(g)
        eight = eights(c)
        terms = first_rows(weight_t, c)
        for i in range(T // 16):
            rows, terms = next_rows(terms, eight)
            hbuf[pl.ds(i * 16, 16), c] = rows.astype(BF16)
        return 0

    def long_spectrum(j):
        spec_l[:, cols(j)] = dot(fl[...], hbuf[:, cols(j)])

    loads[2].wait()
    loads[3].wait()
    lax.fori_loop(0, groups, mode_tables, 0)

    @pl.when(d == 0)
    def _():
        buf[pl.ds(0, K), :] = jnp.zeros((K, C), BF16)

    for i in range(4, 12):
        loads[i].wait()
    fm[...] = fm32[...].astype(BF16)
    gm[...] = gm32[...].astype(BF16)
    for j in range(chunks):
        product(0, j)
    sq_acc[...] = jnp.zeros_like(sq_acc)
    for j in range(chunks):
        spec_m[:, cols(j)] = dot(fm[:, :K], taps[:, cols(j)])
        medium(K, j)
    send_squares(1)
    lax.fori_loop(0, groups, long_taps, 0)
    for i in range(12, 18):
        loads[i].wait()
    fl[...] = fl32[...].astype(BF16)
    gl[...] = gl32[...].astype(BF16)
    take_squares(1)
    lax.fori_loop(0, groups, functools.partial(normed, 1), 0)

    sq_acc[...] = jnp.zeros_like(sq_acc)
    for j in range(chunks):
        @pl.when(d >= 1)
        def _(j=j):
            halo(j).wait_recv()
        medium(0, j)
    send_squares(0)
    rout_copy = pltpu.make_async_copy(rout, rout_h, out_sem.at[chunks])
    rout_copy.start()
    for j in range(chunks):
        long_spectrum(j)
    take_squares(0)

    per = groups // chunks

    def hop(i, j):
        c = cols(j)
        return pltpu.make_async_remote_copy(
            src_ref=st_send.at[i, :, c], dst_ref=st_recv.at[i, :, c],
            send_sem=st_ssem.at[i, j], recv_sem=st_rsem.at[i, j],
            device_id=(lax.rem(d + shifts[i], n), t), device_id_type=MESH)

    def send_state(i, j):
        @pl.when(d + shifts[i] < n)
        def _():
            c = cols(j)
            st_send[i, :, c] = state[:, c].astype(BF16)
            hop(i, j).start()

    def take_state(i, j):
        s = shifts[i]

        @pl.when(d >= s)
        def _():
            c = cols(j)
            rate = rates[:, c]
            near, far = jnp.exp(rate * -float(T * (s - 1))), jnp.exp(rate * -float(T * s))
            hop(i, j).wait_recv()
            arrived = st_recv[i, :, c].astype(F32)
            carry[:, c] += near * arrived
            if i + 1 < steps:
                state[:, c] += far * arrived

    def inside(j):
        c = cols(j)
        y = complex_product(dot(fl[...], v2[:, c]), spec_l[:, c])
        loc[:, c] = dot(gl[...], y) + skip2[:, c] * v2[:, c].astype(F32)

    def finish(g, _):
        c = lane(g)
        eight = eights(c)
        terms = first_rows(carry, c)
        for i in range(T // 16):
            r = pl.ds(i * 16, 16)
            rows, terms = next_rows(terms, eight)
            obuf[r, c] = (q2[r, c].astype(F32) * (loc[r, c] + rows)).astype(BF16)
        return 0

    carry[...] = jnp.zeros_like(carry)
    for j in range(chunks):
        lax.fori_loop(j * per, (j + 1) * per, functools.partial(normed, 0), 0)
        c = cols(j)
        state[:, c] += jnp.exp(rates[:, c] * -float(K)) * low[:, c]
        send_state(0, j)
    waiting = list(range(chunks))
    for i in range(steps - 1):
        for j in range(chunks):
            if j % 2 == 0 and waiting:
                inside(waiting.pop(0))
            take_state(i, j)
            send_state(i + 1, j)
    for j in waiting:
        inside(j)
    for j in range(chunks):
        c = cols(j)
        take_state(steps - 1, j)
        carry[:, c] = carry[:, c] * later_t[:, c]
        lax.fori_loop(j * per, (j + 1) * per, finish, 0)
        pltpu.make_async_copy(obuf.at[:, c], lout_h.at[:, c], out_sem.at[j]).start()

    for j in range(chunks):
        @pl.when(d + 1 < n)
        def _(j=j):
            halo(j).wait_send()
    for i, s in enumerate(shifts):
        @pl.when(d + s < n)
        def _(i=i):
            for j in range(chunks):
                hop(i, j).wait_send()
    rout_copy.wait()
    for j in range(chunks):
        c = cols(j)
        pltpu.make_async_copy(obuf.at[:, c], lout_h.at[:, c], out_sem.at[j]).wait()


def hand_on(a_from, b_from, a_to, b_to, held, in_sem, out_sem):
    pieces = in_sem.shape[1]
    rows = a_from.shape[0] // pieces
    copies = []
    for i in range(pieces):
        for k, (x, y) in enumerate([(a_from, a_to), (b_from, b_to)]):
            r = pl.ds(i * rows, rows)
            copies.append((
                pltpu.make_async_copy(x.at[r], held.at[k, r], in_sem.at[k, i]),
                pltpu.make_async_copy(held.at[k, r], y.at[r], out_sem.at[k, i])))
    for inward, _ in copies:
        inward.start()
    for inward, outward in copies:
        inward.wait()
        outward.start()
    for _, outward in copies:
        outward.wait()


def on_device(n, tp_n, q1, k1, v1, res, taps, skip1, gain, q2, k2, residues, rates, skip2):
    T, C = q1.shape
    K = taps.shape[0]
    M = residues.shape[0]
    assert T == 2 * K and C % CHUNK == 0
    chunks = C // CHUNK
    steps = (n - 1).bit_length()
    fm, gm = half_bin_tables(2 * K, 2 * K, K, 2 * K)
    fl, gl = half_bin_tables(2 * T, T, 0, T)
    hbm = pl.BlockSpec(memory_space=pl.ANY)
    line = pltpu.VMEM((1, C), F32)
    modes = pltpu.VMEM((M, C), F32)
    wide = pltpu.VMEM((T, C), BF16)
    outs = pl.pallas_call(
        functools.partial(kernel, n, tp_n),
        out_shape=[jax.ShapeDtypeStruct((T, C), BF16)] * 2,
        in_specs=[hbm] * 16,
        out_specs=[hbm] * 2,
        scratch_shapes=[
            wide, wide, wide, wide, pltpu.VMEM((K, C), BF16), line, line, wide, wide,
            modes, modes, line,
            pltpu.VMEM(fm.shape, F32), pltpu.VMEM(gm.shape, F32),
            pltpu.VMEM(fl.shape, F32), pltpu.VMEM(gl.shape, F32),
            pltpu.VMEM(fm.shape, BF16), pltpu.VMEM(gm.shape, BF16),
            pltpu.VMEM(fl.shape, BF16), pltpu.VMEM(gl.shape, BF16),
            pltpu.VMEM((T + K, C), BF16),
            pltpu.VMEM((2 * K, C), F32),
            pltpu.VMEM((2 * T, C), F32),
            wide, wide, wide,
            pltpu.VMEM((T, C), F32),
            wide,
            pltpu.VMEM((K, LANES), F32),
            pltpu.VMEM((2, 8, K), F32),
            pltpu.VMEM((2, tp_n - 1, 8, K), F32),
            pltpu.VMEM((K, LANES), F32),
            modes,
            modes,
            modes,
            pltpu.VMEM((8 * M, C), F32),
            pltpu.VMEM((8 * M, C), F32),
            modes,
            modes,
            modes,
            pltpu.VMEM((steps, M, C), BF16),
            pltpu.VMEM((steps, M, C), BF16),
            pltpu.SemaphoreType.DMA((18,)),
            pltpu.SemaphoreType.DMA((chunks + 1,)),
            pltpu.SemaphoreType.DMA((chunks,)),
            pltpu.SemaphoreType.DMA((chunks,)),
            pltpu.SemaphoreType.DMA((2, tp_n - 1)),
            pltpu.SemaphoreType.DMA((2, tp_n - 1)),
            pltpu.SemaphoreType.DMA((steps, chunks)),
            pltpu.SemaphoreType.DMA((steps, chunks)),
        ],
        compiler_params=pltpu.CompilerParams(
            collective_id=0, has_side_effects=True, vmem_limit_bytes=56 * 2**20),
        cost_estimate=pl.CostEstimate(
            flops=2 * 620000 * C, bytes_accessed=10 * T * C * 2, transcendentals=M * C * 16),
    )(q1, k1, v1, res, taps, skip1.reshape(1, C), gain.reshape(1, C), q2, k2, residues, rates,
      skip2.reshape(1, C), jnp.asarray(fm), jnp.asarray(gm), jnp.asarray(fl), jnp.asarray(gl))
    plain = pl.BlockSpec(memory_space=pltpu.HBM)
    return pl.pallas_call(
        hand_on,
        out_shape=[jax.ShapeDtypeStruct((T, C), BF16)] * 2,
        in_specs=[plain] * 2,
        out_specs=[plain] * 2,
        scratch_shapes=[
            pltpu.VMEM((2, T, C), BF16), pltpu.SemaphoreType.DMA((2, 4)), pltpu.SemaphoreType.DMA((2, 4))],
        cost_estimate=pl.CostEstimate(flops=0, bytes_accessed=8 * T * C, transcendentals=0),
    )(*outs)


def solution(mesh):
    rows = P("ctx", "tp")
    in_specs = (
        rows, rows, rows, rows, P(None, "tp"), P("tp"), P("tp"), rows, rows,
        P(None, "tp"), P(None, "tp"), P("tp"),
    )
    return jax.shard_map(
        functools.partial(on_device, mesh.shape["ctx"], mesh.shape["tp"]),
        mesh=mesh, in_specs=in_specs, out_specs=(rows, rows), check_vma=False)
```

```python
import functools

import jax
import jax.numpy as jnp
import ml_dtypes
import numpy as np
from jax import lax
from jax.experimental import pallas as pl
from jax.experimental.pallas import tpu as pltpu
from jax.sharding import PartitionSpec as P

F32 = jnp.float32
BF16 = jnp.bfloat16
MESH = pl.DeviceIdType.MESH
LANES = 128
CHUNK = 512


def half_bin_tables(period, rows_in, out_from, out_to):
    bins = np.arange(period // 2)[:, None] + 0.5
    angle = 2.0 * np.pi / period * bins * np.arange(period)[None, :]
    forward = np.concatenate([np.cos(angle), -np.sin(angle)], axis=0)[:, :rows_in]
    inverse = np.concatenate([np.cos(angle), -np.sin(angle)], axis=0).T[out_from:out_to] * (2.0 / period)
    return [x.astype(ml_dtypes.bfloat16).astype(np.float32) for x in (forward, inverse)]


def dot(left, right):
    return jnp.dot(left, right, preferred_element_type=F32)


def complex_product(x, h):
    half = x.shape[0] // 2
    xr, xi, hr, hi = x[:half], x[half:], h[:half], h[half:]
    return jnp.concatenate([xr * hr - xi * hi, xr * hi + xi * hr], axis=0).astype(BF16)


def kernel(
    n, tp_n,
    q1_h, k1_h, v1_h, res_h, taps_h, skip1_h, gain_h, q2_h, k2_h, residues_h, rates_h, skip2_h,
    fm_h, gm_h, fl_h, gl_h,
    rout, obuf,
    q1, k1, v1, res, taps, skip1, gain, q2, k2, residues, rates, skip2, fm32, gm32, fl32, gl32, fm, gm, fl, gl,
    buf, spec_m, spec_l, hbuf, v2, loc,
    sq_acc, sq_send, sq_recv, scale, eight_t, weight_t, later_t, up_t, down_t, low, state, carry, st_send, st_recv,
    in_sem, halo_send, halo_recv, sq_ssem, sq_rsem, st_ssem, st_rsem,
):
    T, C = q1.shape
    K = taps.shape[0]
    M = residues.shape[0]
    groups = C // LANES
    chunks = C // CHUNK
    steps = (n - 1).bit_length()
    d = lax.axis_index("ctx")
    t = lax.axis_index("tp")

    def lane(g):
        return pl.ds(pl.multiple_of(g * LANES, LANES), LANES)

    def cols(j):
        return pl.ds(j * CHUNK, CHUNK)

    last, top = pl.ds(T - K, K), pl.ds(0, T - K)
    pairs = [
        (k1_h.at[last], k1.at[last]), (v1_h.at[last], v1.at[last]),
        (rates_h, rates), (residues_h, residues), (k1_h.at[top], k1.at[top]), (v1_h.at[top], v1.at[top]),
        (fm_h, fm32), (taps_h, taps), (gm_h, gm32), (skip1_h, skip1), (q1_h, q1), (res_h, res),
        (k2_h, k2), (gain_h, gain), (fl_h, fl32), (gl_h, gl32), (skip2_h, skip2), (q2_h, q2),
    ]
    loads = [pltpu.make_async_copy(a, b, in_sem.at[i]) for i, (a, b) in enumerate(pairs)]
    loads[0].start()
    loads[1].start()

    barrier = pltpu.get_barrier_semaphore()
    shifts = [1 << i for i in range(steps)]
    for s in shifts:
        @pl.when(d + s < n)
        def _(s=s):
            pl.semaphore_signal(barrier, inc=1, device_id=(d + s, t), device_id_type=MESH)

        @pl.when(d >= s)
        def _(s=s):
            pl.semaphore_signal(barrier, inc=1, device_id=(d - s, t), device_id_type=MESH)
    for o in range(1, tp_n):
        pl.semaphore_signal(barrier, inc=1, device_id=(d, lax.rem(t + o, tp_n)), device_id_type=MESH)
    def halo(j):
        c = cols(j)
        return pltpu.make_async_remote_copy(
            src_ref=buf.at[pl.ds(T, K), c], dst_ref=buf.at[pl.ds(0, K), c],
            send_sem=halo_send.at[j], recv_sem=halo_recv.at[j],
            device_id=(lax.rem(d + 1, n), t), device_id_type=MESH)

    def product(row, j):
        c = cols(j)
        r = pl.ds(row, K)
        buf[pl.ds(K + row, K), c] = (k1[r, c].astype(F32) * v1[r, c].astype(F32)).astype(BF16)

    loads[0].wait()
    loads[1].wait()
    for load in loads[2:]:
        load.start()
    for j in range(chunks):
        product(T - K, j)
    peers = tp_n - 1
    for s in shifts:
        peers = peers + (d + s < n).astype(jnp.int32) + (d >= s).astype(jnp.int32)
    pl.semaphore_wait(barrier, peers)
    for j in range(chunks):
        @pl.when(d + 1 < n)
        def _(j=j):
            halo(j).start()
    def medium(row, j):
        c = cols(j)
        r = pl.ds(row, K)
        x = dot(fm[...], buf[pl.ds(row, 2 * K), c])
        filtered = dot(gm[...], complex_product(x, spec_m[:, c]))
        mixed = filtered + skip1[:, c] * buf[pl.ds(K + row, K), c].astype(F32)
        out = (res[r, c].astype(F32) + q1[r, c].astype(F32) * mixed).astype(BF16)
        rout[r, c] = out
        wide = out.astype(F32)
        square = wide * wide
        total = sq_acc[...]
        for i in range(CHUNK // LANES):
            total = total + square[:, i * LANES:(i + 1) * LANES]
        sq_acc[...] = total

    def send_squares(half):
        summed = jnp.sum(sq_acc[...].T, axis=0, keepdims=True)
        sq_send[half] = jnp.broadcast_to(summed, (8, K))
        for o in range(1, tp_n):
            squares(half, o).start()

    def squares(half, o):
        return pltpu.make_async_remote_copy(
            src_ref=sq_send.at[half], dst_ref=sq_recv.at[half, o - 1],
            send_sem=sq_ssem.at[half, o - 1], recv_sem=sq_rsem.at[half, o - 1],
            device_id=(d, lax.rem(t + o, tp_n)), device_id_type=MESH)

    def take_squares(half):
        total = sq_send[half]
        for o in range(1, tp_n):
            squares(half, o).wait()
            total = total + sq_recv[half, o - 1]
        root = lax.rsqrt(total * (1.0 / (C * tp_n)) + 1e-05)
        scale[...] = jnp.concatenate([root] * (K // 8), axis=0).T

    def mode_tables(g, _):
        c = lane(g)
        sub = lax.broadcasted_iota(jnp.int32, (8, LANES), 0).astype(F32)
        rate = rates[:, c]
        eight_t[:, c] = jnp.exp(rate * -8.0)
        weight_t[:, c] = residues[:, c] * jnp.sqrt(rate)
        later_t[:, c] = weight_t[:, c] * jnp.exp(-rate)
        for m in range(M):
            row = jnp.broadcast_to(rates[pl.ds(m, 1), c], (8, LANES))
            up_t[pl.ds(8 * m, 8), c] = jnp.exp(-row * sub)
            down_t[pl.ds(8 * m, 8), c] = jnp.exp(-row * (7.0 - sub))
        return 0

    def eights(c):
        return [jnp.broadcast_to(eight_t[pl.ds(m, 1), c], (8, LANES)) for m in range(M)]

    def first_rows(factor, c):
        return [up_t[pl.ds(8 * m, 8), c] * factor[pl.ds(m, 1), c] for m in range(M)]

    def tree_sum(terms):
        while len(terms) > 1:
            terms = [a + b for a, b in zip(terms[::2], terms[1::2])] + terms[len(terms) // 2 * 2:]
        return terms[0]

    def next_rows(terms, eight):
        top = tree_sum(terms)
        terms = [p * a for p, a in zip(terms, eight)]
        bottom = tree_sum(terms)
        return jnp.concatenate([top, bottom], axis=0), [p * a for p, a in zip(terms, eight)]

    def normed(half, g, _):
        c = lane(g)
        eight = eights(c)
        held = [jnp.zeros((8, LANES), F32)] * M
        for i in range(K // 16):
            r = pl.ds(half * K + i * 16, 16)
            value = (k2[r, c].astype(F32) * rout[r, c].astype(F32) * scale[pl.ds(i * 16, 16), :] * gain[:, c]).astype(BF16)
            v2[r, c] = value
            wide = value.astype(F32)
            held = [h * a + wide[:8] for h, a in zip(held, eight)]
            held = [h * a + wide[8:] for h, a in zip(held, eight)]
        into = low if half == 0 else state
        for m in range(M):
            into[pl.ds(m, 1), c] = jnp.sum(held[m] * down_t[pl.ds(8 * m, 8), c], axis=0, keepdims=True)
        return 0

    def long_taps(g, _):
        c = lane(g)
        eight = eights(c)
        terms = first_rows(weight_t, c)
        for i in range(T // 16):
            rows, terms = next_rows(terms, eight)
            hbuf[pl.ds(i * 16, 16), c] = rows.astype(BF16)
        return 0

    def long_spectrum(j):
        spec_l[:, cols(j)] = dot(fl[...], hbuf[:, cols(j)])

    loads[2].wait()
    loads[3].wait()
    lax.fori_loop(0, groups, mode_tables, 0)

    @pl.when(d == 0)
    def _():
        buf[pl.ds(0, K), :] = jnp.zeros((K, C), BF16)

    for i in range(4, 12):
        loads[i].wait()
    fm[...] = fm32[...].astype(BF16)
    gm[...] = gm32[...].astype(BF16)
    for j in range(chunks):
        product(0, j)
    sq_acc[...] = jnp.zeros_like(sq_acc)
    for j in range(chunks):
        spec_m[:, cols(j)] = dot(fm[:, :K], taps[:, cols(j)])
        medium(K, j)
    send_squares(1)
    lax.fori_loop(0, groups, long_taps, 0)
    for i in range(12, 18):
        loads[i].wait()
    fl[...] = fl32[...].astype(BF16)
    gl[...] = gl32[...].astype(BF16)
    take_squares(1)
    lax.fori_loop(0, groups, functools.partial(normed, 1), 0)

    sq_acc[...] = jnp.zeros_like(sq_acc)
    for j in range(chunks):
        @pl.when(d >= 1)
        def _(j=j):
            halo(j).wait_recv()
        medium(0, j)
    send_squares(0)
    for j in range(chunks):
        long_spectrum(j)
    take_squares(0)

    per = groups // chunks

    def hop(i, j):
        c = cols(j)
        return pltpu.make_async_remote_copy(
            src_ref=st_send.at[i, :, c], dst_ref=st_recv.at[i, :, c],
            send_sem=st_ssem.at[i, j], recv_sem=st_rsem.at[i, j],
            device_id=(lax.rem(d + shifts[i], n), t), device_id_type=MESH)

    def send_state(i, j):
        @pl.when(d + shifts[i] < n)
        def _():
            c = cols(j)
            st_send[i, :, c] = state[:, c].astype(BF16)
            hop(i, j).start()

    def take_state(i, j):
        s = shifts[i]

        @pl.when(d >= s)
        def _():
            c = cols(j)
            rate = rates[:, c]
            near, far = jnp.exp(rate * -float(T * (s - 1))), jnp.exp(rate * -float(T * s))
            hop(i, j).wait_recv()
            arrived = st_recv[i, :, c].astype(F32)
            carry[:, c] += near * arrived
            if i + 1 < steps:
                state[:, c] += far * arrived

    def inside(j):
        c = cols(j)
        y = complex_product(dot(fl[...], v2[:, c]), spec_l[:, c])
        loc[:, c] = dot(gl[...], y) + skip2[:, c] * v2[:, c].astype(F32)

    def finish(g, _):
        c = lane(g)
        eight = eights(c)
        terms = first_rows(carry, c)
        for i in range(T // 16):
            r = pl.ds(i * 16, 16)
            rows, terms = next_rows(terms, eight)
            obuf[r, c] = (q2[r, c].astype(F32) * (loc[r, c] + rows)).astype(BF16)
        return 0

    carry[...] = jnp.zeros_like(carry)
    for j in range(chunks):
        lax.fori_loop(j * per, (j + 1) * per, functools.partial(normed, 0), 0)
        c = cols(j)
        state[:, c] += jnp.exp(rates[:, c] * -float(K)) * low[:, c]
        send_state(0, j)
    waiting = list(range(chunks))
    for i in range(steps - 1):
        for j in range(chunks):
            if j % 2 == 0 and waiting:
                inside(waiting.pop(0))
            take_state(i, j)
            send_state(i + 1, j)
    for j in waiting:
        inside(j)
    for j in range(chunks):
        c = cols(j)
        take_state(steps - 1, j)
        carry[:, c] = carry[:, c] * later_t[:, c]
        lax.fori_loop(j * per, (j + 1) * per, finish, 0)

    for j in range(chunks):
        @pl.when(d + 1 < n)
        def _(j=j):
            halo(j).wait_send()
    for i, s in enumerate(shifts):
        @pl.when(d + s < n)
        def _(i=i):
            for j in range(chunks):
                hop(i, j).wait_send()


def hand_on(a_from, b_from, a_to, b_to, sem):
    pieces = sem.shape[1]
    rows = a_from.shape[0] // pieces
    copies = [
        pltpu.make_async_copy(x.at[pl.ds(i * rows, rows)], y.at[pl.ds(i * rows, rows)], sem.at[k, i])
        for k, (x, y) in enumerate([(a_from, a_to), (b_from, b_to)]) for i in range(pieces)
    ]
    for copy in copies:
        copy.start()
    for copy in copies:
        copy.wait()


def on_device(n, tp_n, q1, k1, v1, res, taps, skip1, gain, q2, k2, residues, rates, skip2):
    T, C = q1.shape
    K = taps.shape[0]
    M = residues.shape[0]
    assert T == 2 * K and C % CHUNK == 0
    chunks = C // CHUNK
    steps = (n - 1).bit_length()
    fm, gm = half_bin_tables(2 * K, 2 * K, K, 2 * K)
    fl, gl = half_bin_tables(2 * T, T, 0, T)
    hbm = pl.BlockSpec(memory_space=pltpu.HBM)
    vmem = pl.BlockSpec(memory_space=pltpu.VMEM)
    line = pltpu.VMEM((1, C), F32)
    modes = pltpu.VMEM((M, C), F32)
    wide = pltpu.VMEM((T, C), BF16)
    outs = pl.pallas_call(
        functools.partial(kernel, n, tp_n),
        out_shape=[pltpu.VMEM((T, C), BF16)] * 2,
        in_specs=[hbm] * 16,
        out_specs=[vmem] * 2,
        scratch_shapes=[
            wide, wide, wide, wide, pltpu.VMEM((K, C), BF16), line, line, wide, wide,
            modes, modes, line,
            pltpu.VMEM(fm.shape, F32), pltpu.VMEM(gm.shape, F32),
            pltpu.VMEM(fl.shape, F32), pltpu.VMEM(gl.shape, F32),
            pltpu.VMEM(fm.shape, BF16), pltpu.VMEM(gm.shape, BF16),
            pltpu.VMEM(fl.shape, BF16), pltpu.VMEM(gl.shape, BF16),
            pltpu.VMEM((T + K, C), BF16),
            pltpu.VMEM((2 * K, C), F32),
            pltpu.VMEM((2 * T, C), F32),
            wide, wide,
            pltpu.VMEM((T, C), F32),
            pltpu.VMEM((K, LANES), F32),
            pltpu.VMEM((2, 8, K), F32),
            pltpu.VMEM((2, tp_n - 1, 8, K), F32),
            pltpu.VMEM((K, LANES), F32),
            modes,
            modes,
            modes,
            pltpu.VMEM((8 * M, C), F32),
            pltpu.VMEM((8 * M, C), F32),
            modes,
            modes,
            modes,
            pltpu.VMEM((steps, M, C), BF16),
            pltpu.VMEM((steps, M, C), BF16),
            pltpu.SemaphoreType.DMA((18,)),
            pltpu.SemaphoreType.DMA((chunks,)),
            pltpu.SemaphoreType.DMA((chunks,)),
            pltpu.SemaphoreType.DMA((2, tp_n - 1)),
            pltpu.SemaphoreType.DMA((2, tp_n - 1)),
            pltpu.SemaphoreType.DMA((steps, chunks)),
            pltpu.SemaphoreType.DMA((steps, chunks)),
        ],
        compiler_params=pltpu.CompilerParams(
            collective_id=0, has_side_effects=True, vmem_limit_bytes=56 * 2**20),
        cost_estimate=pl.CostEstimate(
            flops=2 * 620000 * C, bytes_accessed=10 * T * C * 2, transcendentals=M * C * 16),
    )(q1, k1, v1, res, taps, skip1.reshape(1, C), gain.reshape(1, C), q2, k2, residues, rates,
      skip2.reshape(1, C), jnp.asarray(fm), jnp.asarray(gm), jnp.asarray(fl), jnp.asarray(gl))
    return pl.pallas_call(
        hand_on,
        out_shape=[jax.ShapeDtypeStruct((T, C), BF16)] * 2,
        in_specs=[vmem] * 2,
        out_specs=[hbm] * 2,
        scratch_shapes=[pltpu.SemaphoreType.DMA((2, 4))],
        cost_estimate=pl.CostEstimate(flops=0, bytes_accessed=4 * T * C, transcendentals=0),
    )(*outs)


def solution(mesh):
    rows = P("ctx", "tp")
    in_specs = (
        rows, rows, rows, rows, P(None, "tp"), P("tp"), P("tp"), rows, rows,
        P(None, "tp"), P(None, "tp"), P("tp"),
    )
    return jax.shard_map(
        functools.partial(on_device, mesh.shape["ctx"], mesh.shape["tp"]),
        mesh=mesh, in_specs=in_specs, out_specs=(rows, rows), check_vma=False)
```

```python
import functools

import jax
import jax.numpy as jnp
import ml_dtypes
import numpy as np
from jax import lax
from jax.experimental import pallas as pl
from jax.experimental.pallas import tpu as pltpu
from jax.sharding import PartitionSpec as P

F32 = jnp.float32
BF16 = jnp.bfloat16
MESH = pl.DeviceIdType.MESH
LANES = 128
CHUNK = 512


def half_bin_tables(period, rows_in, out_from, out_to):
    bins = np.arange(period // 2)[:, None] + 0.5
    angle = 2.0 * np.pi / period * bins * np.arange(period)[None, :]
    forward = np.concatenate([np.cos(angle), -np.sin(angle)], axis=0)[:, :rows_in]
    inverse = np.concatenate([np.cos(angle), -np.sin(angle)], axis=0).T[out_from:out_to] * (2.0 / period)
    return [x.astype(ml_dtypes.bfloat16).astype(np.float32) for x in (forward, inverse)]


def dot(left, right):
    return jnp.dot(left, right, preferred_element_type=F32)


def complex_product(x, h):
    half = x.shape[0] // 2
    xr, xi, hr, hi = x[:half], x[half:], h[:half], h[half:]
    return jnp.concatenate([xr * hr - xi * hi, xr * hi + xi * hr], axis=0).astype(BF16)


def kernel(
    n, tp_n,
    q1_h, k1_h, v1_h, res_h, taps_h, skip1_h, gain_h, q2_h, k2_h, residues_h, rates_h, skip2_h,
    fm_h, gm_h, fl_h, gl_h,
    rout, obuf,
    q1, k1, v1, res, taps, skip1, gain, q2, k2, residues, rates, skip2, fm32, gm32, fl32, gl32, fm, gm, fl, gl,
    buf, spec_m, spec_l, hbuf, v2, loc,
    sq_acc, sq_send, sq_recv, scale, eight_t, weight_t, later_t, up_t, down_t, low, state, carry, st_send, st_recv,
    in_sem, halo_send, halo_recv, sq_ssem, sq_rsem, st_ssem, st_rsem,
):
    T, C = q1.shape
    K = taps.shape[0]
    M = residues.shape[0]
    groups = C // LANES
    chunks = C // CHUNK
    steps = (n - 1).bit_length()
    d = lax.axis_index("ctx")
    t = lax.axis_index("tp")

    def lane(g):
        return pl.ds(pl.multiple_of(g * LANES, LANES), LANES)

    def cols(j):
        return pl.ds(j * CHUNK, CHUNK)

    last, top = pl.ds(T - K, K), pl.ds(0, T - K)
    pairs = [
        (k1_h.at[last], k1.at[last]), (v1_h.at[last], v1.at[last]),
        (rates_h, rates), (residues_h, residues), (k1_h.at[top], k1.at[top]), (v1_h.at[top], v1.at[top]),
        (fm_h, fm32), (taps_h, taps), (gm_h, gm32), (skip1_h, skip1), (q1_h, q1), (res_h, res),
        (k2_h, k2), (gain_h, gain), (fl_h, fl32), (gl_h, gl32), (skip2_h, skip2), (q2_h, q2),
    ]
    loads = [pltpu.make_async_copy(a, b, in_sem.at[i]) for i, (a, b) in enumerate(pairs)]
    loads[0].start()
    loads[1].start()

    barrier = pltpu.get_barrier_semaphore()
    shifts = [1 << i for i in range(steps)]
    for s in shifts:
        @pl.when(d + s < n)
        def _(s=s):
            pl.semaphore_signal(barrier, inc=1, device_id=(d + s, t), device_id_type=MESH)

        @pl.when(d >= s)
        def _(s=s):
            pl.semaphore_signal(barrier, inc=1, device_id=(d - s, t), device_id_type=MESH)
    for o in range(1, tp_n):
        pl.semaphore_signal(barrier, inc=1, device_id=(d, lax.rem(t + o, tp_n)), device_id_type=MESH)
    def halo(j):
        c = cols(j)
        return pltpu.make_async_remote_copy(
            src_ref=buf.at[pl.ds(T, K), c], dst_ref=buf.at[pl.ds(0, K), c],
            send_sem=halo_send.at[j], recv_sem=halo_recv.at[j],
            device_id=(lax.rem(d + 1, n), t), device_id_type=MESH)

    def product(row, j):
        c = cols(j)
        r = pl.ds(row, K)
        buf[pl.ds(K + row, K), c] = (k1[r, c].astype(F32) * v1[r, c].astype(F32)).astype(BF16)

    loads[0].wait()
    loads[1].wait()
    for load in loads[2:]:
        load.start()
    for j in range(chunks):
        product(T - K, j)
    peers = tp_n - 1
    for s in shifts:
        peers = peers + (d + s < n).astype(jnp.int32) + (d >= s).astype(jnp.int32)
    pl.semaphore_wait(barrier, peers)
    for j in range(chunks):
        @pl.when(d + 1 < n)
        def _(j=j):
            halo(j).start()
    def medium(row, j):
        c = cols(j)
        r = pl.ds(row, K)
        x = dot(fm[...], buf[pl.ds(row, 2 * K), c])
        filtered = dot(gm[...], complex_product(x, spec_m[:, c]))
        mixed = filtered + skip1[:, c] * buf[pl.ds(K + row, K), c].astype(F32)
        out = (res[r, c].astype(F32) + q1[r, c].astype(F32) * mixed).astype(BF16)
        rout[r, c] = out
        wide = out.astype(F32)
        square = wide * wide
        total = sq_acc[...]
        for i in range(CHUNK // LANES):
            total = total + square[:, i * LANES:(i + 1) * LANES]
        sq_acc[...] = total

    def send_squares(half):
        summed = jnp.sum(sq_acc[...].T, axis=0, keepdims=True)
        sq_send[half] = jnp.broadcast_to(summed, (8, K))
        for o in range(1, tp_n):
            squares(half, o).start()

    def squares(half, o):
        return pltpu.make_async_remote_copy(
            src_ref=sq_send.at[half], dst_ref=sq_recv.at[half, o - 1],
            send_sem=sq_ssem.at[half, o - 1], recv_sem=sq_rsem.at[half, o - 1],
            device_id=(d, lax.rem(t + o, tp_n)), device_id_type=MESH)

    def take_squares(half):
        total = sq_send[half]
        for o in range(1, tp_n):
            squares(half, o).wait()
            total = total + sq_recv[half, o - 1]
        root = lax.rsqrt(total * (1.0 / (C * tp_n)) + 1e-05)
        scale[...] = jnp.concatenate([root] * (K // 8), axis=0).T

    def mode_tables(g, _):
        c = lane(g)
        sub = lax.broadcasted_iota(jnp.int32, (8, LANES), 0).astype(F32)
        rate = rates[:, c]
        eight_t[:, c] = jnp.exp(rate * -8.0)
        weight_t[:, c] = residues[:, c] * jnp.sqrt(rate)
        later_t[:, c] = weight_t[:, c] * jnp.exp(-rate)
        for m in range(M):
            row = jnp.broadcast_to(rates[pl.ds(m, 1), c], (8, LANES))
            up_t[pl.ds(8 * m, 8), c] = jnp.exp(-row * sub)
            down_t[pl.ds(8 * m, 8), c] = jnp.exp(-row * (7.0 - sub))
        return 0

    def eights(c):
        return [jnp.broadcast_to(eight_t[pl.ds(m, 1), c], (8, LANES)) for m in range(M)]

    def first_rows(factor, c):
        return [up_t[pl.ds(8 * m, 8), c] * factor[pl.ds(m, 1), c] for m in range(M)]

    def tree_sum(terms):
        while len(terms) > 1:
            terms = [a + b for a, b in zip(terms[::2], terms[1::2])] + terms[len(terms) // 2 * 2:]
        return terms[0]

    def next_rows(terms, eight):
        top = tree_sum(terms)
        terms = [p * a for p, a in zip(terms, eight)]
        bottom = tree_sum(terms)
        return jnp.concatenate([top, bottom], axis=0), [p * a for p, a in zip(terms, eight)]

    def normed(half, g, _):
        c = lane(g)
        eight = eights(c)
        held = [jnp.zeros((8, LANES), F32)] * M
        for i in range(K // 16):
            r = pl.ds(half * K + i * 16, 16)
            value = (k2[r, c].astype(F32) * rout[r, c].astype(F32) * scale[pl.ds(i * 16, 16), :] * gain[:, c]).astype(BF16)
            v2[r, c] = value
            wide = value.astype(F32)
            held = [h * a + wide[:8] for h, a in zip(held, eight)]
            held = [h * a + wide[8:] for h, a in zip(held, eight)]
        into = low if half == 0 else state
        for m in range(M):
            into[pl.ds(m, 1), c] = jnp.sum(held[m] * down_t[pl.ds(8 * m, 8), c], axis=0, keepdims=True)
        return 0

    def long_taps(g, _):
        c = lane(g)
        eight = eights(c)
        terms = first_rows(weight_t, c)
        for i in range(T // 16):
            rows, terms = next_rows(terms, eight)
            hbuf[pl.ds(i * 16, 16), c] = rows.astype(BF16)
        return 0

    def long_spectrum(j):
        spec_l[:, cols(j)] = dot(fl[...], hbuf[:, cols(j)])

    loads[2].wait()
    loads[3].wait()
    lax.fori_loop(0, groups, mode_tables, 0)

    @pl.when(d == 0)
    def _():
        buf[pl.ds(0, K), :] = jnp.zeros((K, C), BF16)

    for i in range(4, 12):
        loads[i].wait()
    fm[...] = fm32[...].astype(BF16)
    gm[...] = gm32[...].astype(BF16)
    for j in range(chunks):
        product(0, j)
    sq_acc[...] = jnp.zeros_like(sq_acc)
    for j in range(chunks):
        spec_m[:, cols(j)] = dot(fm[:, :K], taps[:, cols(j)])
        medium(K, j)
    send_squares(1)
    lax.fori_loop(0, groups, long_taps, 0)
    for i in range(12, 18):
        loads[i].wait()
    fl[...] = fl32[...].astype(BF16)
    gl[...] = gl32[...].astype(BF16)
    take_squares(1)
    lax.fori_loop(0, groups, functools.partial(normed, 1), 0)

    sq_acc[...] = jnp.zeros_like(sq_acc)
    for j in range(chunks):
        @pl.when(d >= 1)
        def _(j=j):
            halo(j).wait_recv()
        medium(0, j)
    send_squares(0)
    for j in range(chunks):
        long_spectrum(j)
    take_squares(0)

    per = groups // chunks

    def hop(i, j):
        c = cols(j)
        return pltpu.make_async_remote_copy(
            src_ref=st_send.at[i, :, c], dst_ref=st_recv.at[i, :, c],
            send_sem=st_ssem.at[i, j], recv_sem=st_rsem.at[i, j],
            device_id=(lax.rem(d + shifts[i], n), t), device_id_type=MESH)

    def send_state(i, j):
        @pl.when(d + shifts[i] < n)
        def _():
            c = cols(j)
            st_send[i, :, c] = state[:, c].astype(BF16)
            hop(i, j).start()

    def take_state(i, j):
        s = shifts[i]

        @pl.when(d >= s)
        def _():
            c = cols(j)
            rate = rates[:, c]
            near, far = jnp.exp(rate * -float(T * (s - 1))), jnp.exp(rate * -float(T * s))
            hop(i, j).wait_recv()
            arrived = st_recv[i, :, c].astype(F32)
            carry[:, c] += near * arrived
            if i + 1 < steps:
                state[:, c] += far * arrived

    def inside(j):
        c = cols(j)
        y = complex_product(dot(fl[...], v2[:, c]), spec_l[:, c])
        loc[:, c] = dot(gl[...], y) + skip2[:, c] * v2[:, c].astype(F32)

    def finish(g, _):
        c = lane(g)
        eight = eights(c)
        terms = first_rows(carry, c)
        for i in range(T // 16):
            r = pl.ds(i * 16, 16)
            rows, terms = next_rows(terms, eight)
            obuf[r, c] = (q2[r, c].astype(F32) * (loc[r, c] + rows)).astype(BF16)
        return 0

    carry[...] = jnp.zeros_like(carry)
    for j in range(chunks):
        lax.fori_loop(j * per, (j + 1) * per, functools.partial(normed, 0), 0)
        c = cols(j)
        state[:, c] += jnp.exp(rates[:, c] * -float(K)) * low[:, c]
        send_state(0, j)
    waiting = list(range(chunks))
    for i in range(steps - 1):
        for j in range(chunks):
            if j % 2 == 0 and waiting:
                inside(waiting.pop(0))
            take_state(i, j)
            send_state(i + 1, j)
    for j in waiting:
        inside(j)
    for j in range(chunks):
        c = cols(j)
        take_state(steps - 1, j)
        carry[:, c] = carry[:, c] * later_t[:, c]
        lax.fori_loop(j * per, (j + 1) * per, finish, 0)

    for j in range(chunks):
        @pl.when(d + 1 < n)
        def _(j=j):
            halo(j).wait_send()
    for i, s in enumerate(shifts):
        @pl.when(d + s < n)
        def _(i=i):
            for j in range(chunks):
                hop(i, j).wait_send()


def hand_on(a_from, b_from, a_to, b_to, sem):
    pieces = sem.shape[1]
    rows = a_from.shape[0] // pieces
    copies = [
        pltpu.make_async_copy(x.at[pl.ds(i * rows, rows)], y.at[pl.ds(i * rows, rows)], sem.at[k, i])
        for k, (x, y) in enumerate([(a_from, a_to), (b_from, b_to)]) for i in range(pieces)
    ]
    for copy in copies:
        copy.start()
    for copy in copies:
        copy.wait()


def on_device(n, tp_n, q1, k1, v1, res, taps, skip1, gain, q2, k2, residues, rates, skip2):
    T, C = q1.shape
    K = taps.shape[0]
    M = residues.shape[0]
    assert T == 2 * K and C % CHUNK == 0
    chunks = C // CHUNK
    steps = (n - 1).bit_length()
    fm, gm = half_bin_tables(2 * K, 2 * K, K, 2 * K)
    fl, gl = half_bin_tables(2 * T, T, 0, T)
    hbm = pl.BlockSpec(memory_space=pltpu.HBM)
    vmem = pl.BlockSpec(memory_space=pltpu.VMEM)
    line = pltpu.VMEM((1, C), F32)
    modes = pltpu.VMEM((M, C), F32)
    wide = pltpu.VMEM((T, C), BF16)
    outs = pl.pallas_call(
        functools.partial(kernel, n, tp_n),
        out_shape=[pltpu.VMEM((T, C), BF16)] * 2,
        in_specs=[hbm] * 16,
        out_specs=[vmem] * 2,
        scratch_shapes=[
            wide, wide, wide, wide, pltpu.VMEM((K, C), BF16), line, line, wide, wide,
            modes, modes, line,
            pltpu.VMEM(fm.shape, F32), pltpu.VMEM(gm.shape, F32),
            pltpu.VMEM(fl.shape, F32), pltpu.VMEM(gl.shape, F32),
            pltpu.VMEM(fm.shape, BF16), pltpu.VMEM(gm.shape, BF16),
            pltpu.VMEM(fl.shape, BF16), pltpu.VMEM(gl.shape, BF16),
            pltpu.VMEM((T + K, C), BF16),
            pltpu.VMEM((2 * K, C), F32),
            pltpu.VMEM((2 * T, C), F32),
            wide, wide,
            pltpu.VMEM((T, C), F32),
            pltpu.VMEM((K, LANES), F32),
            pltpu.VMEM((2, 8, K), F32),
            pltpu.VMEM((2, tp_n - 1, 8, K), F32),
            pltpu.VMEM((K, LANES), F32),
            modes,
            modes,
            modes,
            pltpu.VMEM((8 * M, C), F32),
            pltpu.VMEM((8 * M, C), F32),
            modes,
            modes,
            modes,
            pltpu.VMEM((steps, M, C), BF16),
            pltpu.VMEM((steps, M, C), BF16),
            pltpu.SemaphoreType.DMA((18,)),
            pltpu.SemaphoreType.DMA((chunks,)),
            pltpu.SemaphoreType.DMA((chunks,)),
            pltpu.SemaphoreType.DMA((2, tp_n - 1)),
            pltpu.SemaphoreType.DMA((2, tp_n - 1)),
            pltpu.SemaphoreType.DMA((steps, chunks)),
            pltpu.SemaphoreType.DMA((steps, chunks)),
        ],
        compiler_params=pltpu.CompilerParams(
            collective_id=0, has_side_effects=True, vmem_limit_bytes=56 * 2**20),
        cost_estimate=pl.CostEstimate(
            flops=2 * 620000 * C, bytes_accessed=10 * T * C * 2, transcendentals=M * C * 16),
    )(q1, k1, v1, res, taps, skip1.reshape(1, C), gain.reshape(1, C), q2, k2, residues, rates,
      skip2.reshape(1, C), jnp.asarray(fm), jnp.asarray(gm), jnp.asarray(fl), jnp.asarray(gl))
    return pl.pallas_call(
        hand_on,
        out_shape=[jax.ShapeDtypeStruct((T, C), BF16)] * 2,
        in_specs=[vmem] * 2,
        out_specs=[hbm] * 2,
        scratch_shapes=[pltpu.SemaphoreType.DMA((2, 4))],
        compiler_params=pltpu.CompilerParams(vmem_limit_bytes=4 * 2**20),
        cost_estimate=pl.CostEstimate(flops=0, bytes_accessed=4 * T * C, transcendentals=0),
    )(*outs)


def solution(mesh):
    rows = P("ctx", "tp")
    in_specs = (
        rows, rows, rows, rows, P(None, "tp"), P("tp"), P("tp"), rows, rows,
        P(None, "tp"), P(None, "tp"), P("tp"),
    )
    return jax.shard_map(
        functools.partial(on_device, mesh.shape["ctx"], mesh.shape["tp"]),
        mesh=mesh, in_specs=in_specs, out_specs=(rows, rows), check_vma=False)
```
